128 devices in a mesh: grp: 4 (over y_hi, core), row: 8 (over y_lo, z), col: 4 (over x).
Axes of the slice: x: 4, y: 4 (y_hi: 2, y_lo: 2; y = y_hi * 2 + y_lo), z: 4, core: 2. Of those that a mesh axis runs over, the one named last changes fastest.
Arguments:
- density: bfloat16 [1024, 15, 128, 128], P(('grp', 'row', 'col')), may hold values from -0.29882812 to 0.29882812
- block_mask: int32 [1024, 15], P(('grp', 'row', 'col')), may hold values 0 or 1
- orbital_cell: int32 [131072], P(('grp', 'row', 'col')), may hold values from 0 to 16383
- slab_of_device: int32 [128], replicated, may hold values from 0 to 127, each once
- positions: float32 [3, 65536], P(None, ('grp', 'row', 'col')), may hold values from 0 to 1
- charges: float32 [65536], P(('grp', 'row', 'col')), may hold values from -3 to 3
Outputs:
- new_density: bfloat16 [1024, 15, 128, 128], P(('grp', 'row', 'col'))
- energies: float32 [65536], P(('grp', 'row', 'col'))
The draws below stay inside these ranges and needn't reach their ends.
Inputs may be any that keep to these rules, and one draw needn't show every extreme that they name: `orbital_cell`: cell numbers lie within one slab of 1 planes. `slab_of_device`: a permutation of the slabs.
All inputs are finite; a program needn't handle non-finite values. No bound on the sum of `block_mask` on one device may be relied on, other than what follows from the above.
Results may differ from the reference program's by a relative error of at most 0.0031.
Values may be sent and summed in bfloat16 or wider, within the bound.
A program may use at most 128 MiB of HBM per device.

```python
import jax
import jax.numpy as jnp
from jax import lax

BS = 128
BAND = 7
SLOTS = 15
ROWS_DEV = 8
NBLOCKS = 1024
ORBITALS = 131072
PLANES_DEV = 1
GRID_Y = 128
GRID_Z = 128
GRID_X = 128
ATOMS = 65536
N_GRP = 4
N_ROW = 8
N_COL = 4


def with_ends(drawn, stream_key, smallest, largest):
    shape = drawn.shape
    place = [jax.random.randint(jax.random.fold_in(stream_key, axis), (), 0, shape[axis]) for axis in range(len(shape))]
    drawn = drawn.at[tuple(place)].set(smallest)
    longest = shape.index(max(shape))
    place[longest] = (place[longest] + 1) % shape[longest]
    return drawn.at[tuple(place)].set(largest)


def level_of(rng, extent, pieces, least, high):
    gain = 1.0
    for position, shards_of in pieces:
        steps = jax.random.uniform(jax.random.fold_in(jax.random.fold_in(rng, 6), position), (shards_of,), jnp.float32, least / len(pieces), high / len(pieces))
        gain = gain * jnp.repeat(jnp.exp(steps), extent[position] // shards_of).reshape((-1,) + (1,) * (len(extent) - 1 - position))
    return gain


def noise(stream_key, shape, deviation, reach, shards=(), held_as=jnp.bfloat16):
    factor_of = level_of(stream_key, shape, shards, -0.22, 0.18) if shards else 1.0
    entries = jax.random.normal(stream_key, shape, jnp.float32) * deviation * factor_of
    return jnp.minimum(jnp.maximum(entries, -reach), reach).astype(held_as)


def setup_inputs(seed: int = 0) -> dict:
    streams_of = jax.random.split(jax.random.key(seed), 7)
    density = noise(streams_of[0], (NBLOCKS, SLOTS, BS, BS), 0.05, 0.29882812, ((0, 128),))
    block_mask = with_ends((jax.random.randint(streams_of[1], (NBLOCKS, SLOTS), 0, 4) < 3).astype(jnp.int32), jax.random.fold_in(streams_of[1], 1), 0, 1)
    orbital_cell = with_ends(jax.random.randint(streams_of[2], (ORBITALS,), 0, PLANES_DEV * GRID_Y * GRID_Z), jax.random.fold_in(streams_of[2], 1), 0, (PLANES_DEV * GRID_Y * GRID_Z) - 1).astype(jnp.int32)
    slab_of_device = jax.random.permutation(streams_of[3], N_GRP * N_ROW * N_COL).astype(jnp.int32)
    positions = jnp.clip(1.0 * jax.random.uniform(streams_of[4], (3, ATOMS), jnp.float32) ** level_of(streams_of[4], (3, ATOMS), ((1, 128),), -0.2, 0.2), 0.0, 1.0)
    charges = noise(streams_of[5], (ATOMS,), 0.5, 3.0, ((0, 128),), jnp.float32)
    return dict(density=density, block_mask=block_mask, orbital_cell=orbital_cell, slab_of_device=slab_of_device, positions=positions, charges=charges)


SPREAD = 2.0
COUPLE = 0.5
DENSITY_SCALE = 0.05


def gaussian(centre, points):
    offset = points[:, None] - centre[None, :]
    return jnp.exp(-offset * offset / (2.0 * SPREAD * SPREAD))


def atom_tables(positions, grid_x):
    height = jnp.arange(GRID_Y, dtype=jnp.float32)
    depth = jnp.arange(GRID_Z, dtype=jnp.float32)
    return positions[0] * grid_x, gaussian(positions[1] * GRID_Y, height), gaussian(positions[2] * GRID_Z, depth)


def plane_potential(plane_id, xcoord, along_y, along_z, charges):
    weight = gaussian(xcoord, plane_id.astype(jnp.float32)[None])[0] * charges
    return jnp.dot(along_y * weight[None, :], along_z.T, precision=lax.Precision.HIGHEST)


def plane_energy(rho_plane, plane_id, xcoord, along_y, along_z):
    weight = gaussian(xcoord, plane_id.astype(jnp.float32)[None])[0]
    inner_sum = jnp.dot(rho_plane, along_z, precision=lax.Precision.HIGHEST)
    return weight * jnp.sum(inner_sum * along_y, axis=0)


def make_work(density, valid_blocks, shifts):
    masked = density * valid_blocks.astype(jnp.bfloat16)[:, :, None, None]
    identity = jnp.eye(BS, dtype=jnp.float32)
    centre_block = (density[:, BAND].astype(jnp.float32) - shifts[:, :, None] * identity[None]) * valid_blocks[:, BAND][:, None, None]
    return masked.at[:, BAND].set(centre_block.astype(jnp.bfloat16))


def band_square(padded, number):
    results = []
    for slot in range(SLOTS):
        lowest = max(0, slot - BAND)
        highest = min(SLOTS - 1, slot + BAND)
        left_side = padded[BAND:BAND + number, lowest:highest + 1].astype(jnp.float32)
        right_side = jnp.stack([padded[shift_id:shift_id + number, slot - shift_id + BAND] for shift_id in range(lowest, highest + 1)], axis=1).astype(jnp.float32)
        results.append(jnp.einsum("raij,rajk->rik", left_side, right_side))
    return jnp.stack(results, axis=1)


def reference(density, block_mask, orbital_cell, slab_of_device, positions, charges):
    members = NBLOCKS // ROWS_DEV
    xcoord, along_y, along_z = atom_tables(positions, GRID_X)
    plane_ids = jnp.arange(GRID_X, dtype=jnp.int32)
    potential = lax.map(lambda plane_id: plane_potential(plane_id, xcoord, along_y, along_z, charges), plane_ids)
    cells_here = PLANES_DEV * GRID_Y * GRID_Z
    orbital_ids = jnp.arange(ORBITALS, dtype=jnp.int32)
    owners = orbital_ids // (ROWS_DEV * BS)
    global_cell = (slab_of_device[owners] * cells_here + orbital_cell).astype(jnp.int32)
    shifts = (COUPLE * potential.reshape(-1)[global_cell]).reshape(NBLOCKS, BS)
    row_ids = jnp.arange(NBLOCKS, dtype=jnp.int32)
    columns = row_ids[:, None] + jnp.arange(SLOTS, dtype=jnp.int32)[None, :] - BAND
    inside = ((columns >= 0) & (columns < NBLOCKS)).astype(jnp.int32)
    valid_blocks = (block_mask * inside).astype(jnp.float32)
    padded_density = jnp.pad(density, ((BAND, BAND), (0, 0), (0, 0), (0, 0)))
    padded_valid = jnp.pad(valid_blocks, ((BAND, BAND), (0, 0)))
    padded_shift = jnp.pad(shifts, ((BAND, BAND), (0, 0)))

    def one_panel(panel):
        offset = (panel * ROWS_DEV).astype(jnp.int32)
        rows_density = lax.dynamic_slice_in_dim(padded_density, offset, ROWS_DEV + 2 * BAND, 0)
        rows_valid = lax.dynamic_slice_in_dim(padded_valid, offset, ROWS_DEV + 2 * BAND, 0)
        rows_shift = lax.dynamic_slice_in_dim(padded_shift, offset, ROWS_DEV + 2 * BAND, 0)
        work = make_work(rows_density, rows_valid, rows_shift)
        squared = band_square(work, ROWS_DEV)
        own = work[BAND:BAND + ROWS_DEV].astype(jnp.float32)
        panel_valid = rows_valid[BAND:BAND + ROWS_DEV]
        return (panel_valid[:, :, None, None] * (2.0 * own - squared)).astype(jnp.bfloat16)

    new_density = lax.map(one_panel, jnp.arange(members, dtype=jnp.int32)).reshape(NBLOCKS, SLOTS, BS, BS)
    diagonal_values = jnp.diagonal(new_density[:, BAND], axis1=1, axis2=2).astype(jnp.float32).reshape(-1) * DENSITY_SCALE
    grid_density = jnp.zeros((GRID_X * GRID_Y * GRID_Z,), jnp.float32).at[global_cell].add(diagonal_values)
    grid_density = grid_density.reshape(GRID_X, GRID_Y, GRID_Z)

    def add_plane(running, plane_id):
        return running + plane_energy(grid_density[plane_id], plane_id, xcoord, along_y, along_z), None

    summed, unused = lax.scan(add_plane, jnp.zeros((ATOMS,), jnp.float32), plane_ids)
    return new_density, charges * summed
```

```python
import functools
import math

import jax
import jax.numpy as jnp
from jax import lax
from jax.experimental import pallas as pl
from jax.experimental.pallas import tpu as pltpu
from jax.sharding import PartitionSpec as P

BS = 128
BAND = 7
SLOTS = 15
ROWS = 8
NBLOCKS = 1024
DEVICES = 128
GRID = 128
SPAN = ROWS * BS
GROUP = 32
RING = 4
ATOMS_DEV = 512
ATOMS_HERE = GROUP * ATOMS_DEV

COUPLE = 0.5
DENSITY_SCALE = 0.05
ROOT = math.sqrt(math.log2(math.e) / 8.0)

MESH = pl.DeviceIdType.MESH
F32 = jnp.float32
BF16 = jnp.bfloat16


def dot(a, b):
    return jnp.dot(a, b, preferred_element_type=F32)


def dot_nt(a, b):
    return lax.dot_general(a, b, (((1,), (1,)), ((), ())), preferred_element_type=F32)


def bell(points, centre):
    offset = points - centre
    return jnp.exp2(-(offset * offset))


def kernel(
    density, mask, slabs, cells, atoms_in, new_density, energies,
    dens, left, right, s_next, s_prev, pu_out, pd_out, pu_in, pd_in,
    atoms, tab_y, tab_z, lhs, pot_acc, pot_out, pot_in, rho, e_out, e_in,
    dens_sem, out_sem, gather_sem, own_sem, halo_send, halo_recv, part_send, part_recv,
    pot_send, pot_recv, rho_send, rho_recv, en_send, en_recv,
):
    g, r, c = lax.axis_index("grp"), lax.axis_index("row"), lax.axis_index("col")
    me = (g * 8 + r) * 4 + c
    mine = g * 8 + r

    def coords(index):
        return (index // 32, (index // 4) % 8, index % 4)

    after = coords((me + 1) % DEVICES)
    before = coords((me + DEVICES - 1) % DEVICES)

    def peer(k):
        slot = (mine + k) % GROUP
        return slot, (slot // 8, slot % 8, c)

    loads = [
        pltpu.make_async_copy(density.at[i], dens.at[i], dens_sem.at[i]) for i in range(ROWS)
    ]
    for load in loads:
        load.start()

    barrier = pltpu.get_barrier_semaphore()

    @pl.loop(1, GROUP)
    def _(k):
        pl.semaphore_signal(barrier, inc=1, device_id=peer(k)[1], device_id_type=MESH)

    for k in range(1, RING):
        pl.semaphore_signal(barrier, inc=1, device_id=(g, r, (c + k) % RING), device_id_type=MESH)
    pl.semaphore_signal(barrier, inc=1, device_id=after, device_id_type=MESH)
    pl.semaphore_signal(barrier, inc=1, device_id=before, device_id_type=MESH)
    pl.semaphore_wait(barrier, GROUP - 1 + RING - 1 + 2)

    own = pltpu.make_async_copy(atoms_in, atoms.at[mine], own_sem)
    own.start()

    @pl.loop(1, GROUP)
    def _(k):
        pltpu.make_async_remote_copy(
            atoms_in, atoms.at[mine], gather_sem.at[0], gather_sem.at[1],
            device_id=peer(k)[1], device_id_type=MESH,
        ).start()

    zero = jnp.zeros((BS, BS), BF16)
    for a in range(0, ROWS, 2):
        for i, j in ((a, a), (a, a + 1), (a + 1, a), (a + 1, a + 1)):
            if j >= i:
                left[i * BS:(i + 1) * BS, 2 * SPAN + j * BS:2 * SPAN + (j + 1) * BS] = zero
                right[i * BS:(i + 1) * BS, j * BS:(j + 1) * BS] = zero
            if j <= i:
                left[i * BS:(i + 1) * BS, j * BS:(j + 1) * BS] = zero
                right[2 * SPAN + i * BS:2 * SPAN + (i + 1) * BS, j * BS:(j + 1) * BS] = zero

    def valid(i, s):
        column = me * ROWS + (i + s - BAND)
        inside = jnp.logical_and(column >= 0, column < NBLOCKS)
        return (mask[i, s] * inside.astype(jnp.int32)).astype(F32)

    to_next, to_prev = [], []
    for i in range(ROWS):
        loads[i].wait()
        for s in range(SLOTS):
            k = i + s + 1
            block = (dens[i, s].astype(F32) * valid(i, s)).astype(BF16)
            left[i * BS:(i + 1) * BS, k * BS:(k + 1) * BS] = block
            if ROWS <= k < 2 * ROWS:
                right[SPAN + i * BS:SPAN + (i + 1) * BS, (k - ROWS) * BS:(k - ROWS + 1) * BS] = block
        here = pl.ds(i * BS, BS)
        if i > 0:
            copy = pltpu.make_async_remote_copy(
                left.at[here, pl.ds(2 * SPAN, i * BS)], right.at[here, pl.ds(0, i * BS)],
                halo_send.at[0, i], halo_recv.at[0, i], device_id=after, device_id_type=MESH,
            )
            copy.start()
            to_next.append(copy)
        if i < ROWS - 1:
            there = pl.ds((i + 1) * BS, (ROWS - 1 - i) * BS)
            copy = pltpu.make_async_remote_copy(
                left.at[here, there], right.at[pl.ds(2 * SPAN + i * BS, BS), there],
                halo_send.at[1, i], halo_recv.at[1, i], device_id=before, device_id_type=MESH,
            )
            copy.start()
            to_prev.append(copy)

    own.wait()
    others = atoms.at[pl.ds(0, GROUP - 1)]
    pltpu.make_async_copy(others, others, gather_sem.at[0]).wait()
    pltpu.make_async_copy(others, others, gather_sem.at[1]).wait()

    points = lax.broadcasted_iota(jnp.int32, (GRID, BS), 0).astype(F32) * ROOT
    planes = [slabs[(me - c) + p].astype(F32) * ROOT for p in range(RING)]
    pot_acc[...] = jnp.zeros_like(pot_acc)

    @pl.loop(0, GROUP)
    def _(slot):
        base = pl.multiple_of(slot * ATOMS_DEV, ATOMS_DEV)
        for j in range(4):
            at = pl.ds(base + j * BS, BS)
            centre = [atoms[slot, pl.ds(4 * d + j, 1), :] * (GRID * ROOT) for d in range(3)]
            charge = atoms[slot, pl.ds(12 + j, 1), :]
            along_y = bell(points, centre[1])
            high = along_y.astype(BF16)
            tab_y[0:GRID, at] = high
            tab_y[GRID:2 * GRID, at] = (along_y - high.astype(F32)).astype(BF16)
            along_z = bell(points, centre[2])
            tab_z[:, at] = along_z
            for p in range(RING):
                weight = bell(planes[p], centre[0]) * charge
                lhs[p * GRID:(p + 1) * GRID, j * BS:(j + 1) * BS] = (along_z * weight).astype(BF16)
        pot_acc[...] += dot_nt(lhs[...], tab_y[:, pl.ds(base, ATOMS_DEV)])

    for p in range(RING):
        part = pot_acc[p * GRID:(p + 1) * GRID, 0:GRID] + pot_acc[p * GRID:(p + 1) * GRID, GRID:2 * GRID]
        pot_out[p] = part
    pot_copies = []
    for k in range(1, RING):
        target = (c + k) % RING
        copy = pltpu.make_async_remote_copy(
            pot_out.at[target], pot_in.at[k], pot_send.at[k], pot_recv.at[k],
            device_id=(g, r, target), device_id_type=MESH,
        )
        copy.start()
        pot_copies.append(copy)
    potential = pot_out[c]
    for k, copy in zip(range(1, RING), pot_copies):
        copy.wait()
        potential = potential + pot_in[k]

    high = potential.astype(BF16)
    both = jnp.concatenate([high, (potential - high.astype(F32)).astype(BF16)], axis=1)
    cell_y = lax.shift_right_logical(cells[...], 7)
    cell_z = jnp.bitwise_and(cells[...], GRID - 1)
    height = lax.broadcasted_iota(jnp.int32, (GRID, BS), 0)
    eye = (height == lax.broadcasted_iota(jnp.int32, (GRID, BS), 1)).astype(F32)

    def hot(cell, i):
        return (height == cell[i:i + 1, :]).astype(F32)

    for i in range(ROWS):
        hot_y = hot(cell_y, i).astype(BF16)
        rows = dot(both, jnp.concatenate([hot_y, hot_y], axis=0))
        shift = COUPLE * jnp.sum(rows * hot(cell_z, i), axis=0, keepdims=True)
        block = ((dens[i, BAND].astype(F32) - shift * eye) * valid(i, BAND)).astype(BF16)
        left[i * BS:(i + 1) * BS, SPAN + i * BS:SPAN + (i + 1) * BS] = block
        right[SPAN + i * BS:SPAN + (i + 1) * BS, i * BS:(i + 1) * BS] = block

    for copy in to_next:
        copy.wait()
    for copy in to_prev:
        copy.wait()

    for a in range(0, ROWS, 2):
        rows = slice(a * BS, (a + 2) * BS)
        depth = (a + 2) * BS
        pu_out[rows, 0:depth] = dot(
            right[rows, 0:depth], right[SPAN:SPAN + depth, 0:depth]
        ).astype(BF16)
        pd_out[rows, a * BS:SPAN] = dot(
            right[2 * SPAN + a * BS:2 * SPAN + (a + 2) * BS, a * BS:SPAN],
            right[SPAN + a * BS:2 * SPAN, a * BS:SPAN],
        ).astype(BF16)
    parts = []
    for i in range(ROWS):
        here = pl.ds(i * BS, BS)
        if i > 0:
            there = pl.ds(0, i * BS)
            copy = pltpu.make_async_remote_copy(
                pu_out.at[here, there], pu_in.at[here, there],
                part_send.at[0, i], part_recv.at[0, i], device_id=before, device_id_type=MESH,
            )
            copy.start()
            parts.append(copy)
        if i < ROWS - 1:
            there = pl.ds((i + 1) * BS, (ROWS - 1 - i) * BS)
            copy = pltpu.make_async_remote_copy(
                pd_out.at[here, there], pd_in.at[here, there],
                part_send.at[1, i], part_recv.at[1, i], device_id=after, device_id_type=MESH,
            )
            copy.start()
            parts.append(copy)

    def middle(a, b):
        first, last = max(a, b) + 1, min(a, b) + 16
        window = slice(first * BS, (last + 1) * BS)
        total = dot(left[a * BS:(a + 2) * BS, window], right[window, b * BS:(b + 2) * BS])
        for i in (a, a + 1):
            for j in (b, b + 1):
                s = j - i + BAND
                held = left[i * BS:(i + 1) * BS, SPAN + j * BS:SPAN + (j + 1) * BS].astype(F32)
                square = total[(i - a) * BS:(i - a + 1) * BS, (j - b) * BS:(j - b + 1) * BS]
                dens[i, s] = ((2.0 * held - square) * valid(i, s)).astype(BF16)

    for a in range(0, ROWS, 2):
        middle(a, a)

    grid_here = jnp.zeros((GRID, GRID), F32)
    for i in range(ROWS):
        diagonal = jnp.sum(dens[i, BAND].astype(F32) * eye, axis=0, keepdims=True)
        spread = (hot(cell_z, i) * diagonal).astype(BF16)
        grid_here = grid_here + dot_nt(spread, hot(cell_y, i).astype(BF16))
    rho[0] = grid_here.astype(BF16)
    rho_copies = []
    for k in range(1, RING):
        copy = pltpu.make_async_remote_copy(
            rho.at[0], rho.at[k], rho_send.at[k], rho_recv.at[k],
            device_id=(g, r, (c + k) % RING), device_id_type=MESH,
        )
        copy.start()
        rho_copies.append(copy)

    for a in range(0, ROWS, 2):
        for b in range(0, ROWS, 2):
            if a != b:
                middle(a, b)
    for b in range(0, ROWS, 2):
        columns = slice(b * BS, (b + 2) * BS)
        rows = slice((b + 1) * BS, SPAN)
        s_next[rows, columns] = dot(
            left[rows, SPAN + b * BS:2 * SPAN],
            left[b * BS:SPAN, 2 * SPAN + b * BS:2 * SPAN + (b + 2) * BS],
        )
        rows = slice(0, (b + 1) * BS)
        s_prev[rows, columns] = dot(
            left[rows, SPAN:SPAN + (b + 2) * BS], left[0:(b + 2) * BS, b * BS:(b + 2) * BS]
        )

    for copy in rho_copies:
        copy.wait()

    order = [lax.rem(c - k + RING, RING) for k in range(RING)]
    mine_planes = [slabs[(me - c) + order[k]].astype(F32) * ROOT for k in range(RING)]
    weights = jnp.concatenate([rho[k] for k in range(RING)], axis=0)
    lhs[:, 0:GRID] = weights
    lhs[:, GRID:2 * GRID] = weights

    @pl.loop(0, GROUP)
    def _(k):
        slot = (mine + 1 + k) % GROUP
        base = pl.multiple_of(slot * ATOMS_DEV, ATOMS_DEV)
        inner = dot(lhs[:, 0:2 * GRID], tab_y[:, pl.ds(base, ATOMS_DEV)])
        for j in range(4):
            at = pl.ds(base + j * BS, BS)
            centre = atoms[slot, pl.ds(j, 1), :] * (GRID * ROOT)
            along_z = tab_z[:, at]
            total = jnp.zeros((1, BS), F32)
            for p in range(RING):
                piece = inner[p * GRID:(p + 1) * GRID, j * BS:(j + 1) * BS]
                total += bell(mine_planes[p], centre) * jnp.sum(piece * along_z, axis=0, keepdims=True)
            e_out[slot, pl.ds(j, 1), :] = total

        @pl.when(k < GROUP - 1)
        def _():
            pltpu.make_async_remote_copy(
                e_out.at[slot], e_in.at[mine], en_send, en_recv,
                device_id=(slot // 8, slot % 8, c), device_id_type=MESH,
            ).start()

    e_in[mine] = e_out[mine]

    for copy in parts:
        copy.wait()
    for i in range(ROWS):
        here = slice(i * BS, (i + 1) * BS)
        for j in range(ROWS):
            there = slice(j * BS, (j + 1) * BS)
            if j < i:
                s = j - i + SLOTS
                held = left[here, 2 * SPAN + j * BS:2 * SPAN + (j + 1) * BS].astype(F32)
                square = s_next[here, there] + pu_in[here, there].astype(F32)
                dens[i, s] = ((2.0 * held - square) * valid(i, s)).astype(BF16)
            if j > i:
                s = j - i - 1
                held = left[here, there].astype(F32)
                square = s_prev[here, there] + pd_in[here, there].astype(F32)
                dens[i, s] = ((2.0 * held - square) * valid(i, s)).astype(BF16)
        pltpu.make_async_copy(dens.at[i], new_density.at[i], out_sem.at[i]).start()

    others = e_out.at[pl.ds(0, GROUP - 1)]
    pltpu.make_async_copy(others, others, en_send).wait()
    pltpu.make_async_copy(others, others, en_recv).wait()
    energies[...] = jnp.sum(e_in[...], axis=0) * DENSITY_SCALE * atoms[mine, pl.ds(12, 4), :]
    for i in range(ROWS):
        pltpu.make_async_copy(dens.at[i], new_density.at[i], out_sem.at[i]).wait()


def on_device(density, block_mask, orbital_cell, slab_of_device, positions, charges):
    atoms = jnp.concatenate([positions.reshape(12, BS), charges.reshape(4, BS)], axis=0)
    dma = pltpu.SemaphoreType.DMA
    new_density, energies = pl.pallas_call(
        kernel,
        out_shape=(
            jax.ShapeDtypeStruct((ROWS, SLOTS, BS, BS), BF16),
            jax.ShapeDtypeStruct((4, BS), F32),
        ),
        in_specs=[
            pl.BlockSpec(memory_space=pl.ANY),
            pl.BlockSpec(memory_space=pltpu.SMEM),
            pl.BlockSpec(memory_space=pltpu.SMEM),
            pl.BlockSpec(memory_space=pltpu.VMEM),
            pl.BlockSpec(memory_space=pltpu.VMEM),
        ],
        out_specs=(pl.BlockSpec(memory_space=pl.ANY), pl.BlockSpec(memory_space=pltpu.VMEM)),
        scratch_shapes=[
            pltpu.VMEM((ROWS, SLOTS, BS, BS), BF16),
            pltpu.VMEM((SPAN, 3 * SPAN), BF16),
            pltpu.VMEM((3 * SPAN, SPAN), BF16),
            pltpu.VMEM((SPAN, SPAN), F32),
            pltpu.VMEM((SPAN, SPAN), F32),
            pltpu.VMEM((SPAN, SPAN), BF16),
            pltpu.VMEM((SPAN, SPAN), BF16),
            pltpu.VMEM((SPAN, SPAN), BF16),
            pltpu.VMEM((SPAN, SPAN), BF16),
            pltpu.VMEM((GROUP, 16, BS), F32),
            pltpu.VMEM((2 * GRID, ATOMS_HERE), BF16),
            pltpu.VMEM((GRID, ATOMS_HERE), F32),
            pltpu.VMEM((RING * GRID, ATOMS_DEV), BF16),
            pltpu.VMEM((RING * GRID, 2 * GRID), F32),
            pltpu.VMEM((RING, GRID, GRID), F32),
            pltpu.VMEM((RING, GRID, GRID), F32),
            pltpu.VMEM((RING, GRID, GRID), BF16),
            pltpu.VMEM((GROUP, 4, BS), F32),
            pltpu.VMEM((GROUP, 4, BS), F32),
            dma((ROWS,)),
            dma((ROWS,)),
            dma((2,)),
            dma,
            dma((2, ROWS)),
            dma((2, ROWS)),
            dma((2, ROWS)),
            dma((2, ROWS)),
            dma((RING,)),
            dma((RING,)),
            dma((RING,)),
            dma((RING,)),
            dma,
            dma,
        ],
        compiler_params=pltpu.CompilerParams(
            collective_id=0, has_side_effects=True, vmem_limit_bytes=60 * 1024 * 1024
        ),
        cost_estimate=pl.CostEstimate(flops=10**10, bytes_accessed=10**7, transcendentals=4 * 10**6),
        name="purify",
    )(density, block_mask, slab_of_device, orbital_cell.reshape(ROWS, BS), atoms)
    return new_density, energies.reshape(ATOMS_DEV)


def solution(mesh):
    in_specs = (
        P(("grp", "row", "col"), None, None, None),
        P(("grp", "row", "col"), None),
        P(("grp", "row", "col")),
        P(),
        P(None, ("grp", "row", "col")),
        P(("grp", "row", "col")),
    )
    out_specs = (P(("grp", "row", "col"), None, None, None), P(("grp", "row", "col")))
    return jax.shard_map(
        on_device, mesh=mesh, in_specs=in_specs, out_specs=out_specs, check_vma=False
    )
```

```python
import functools
import math

import jax
import jax.numpy as jnp
from jax import lax
from jax.experimental import pallas as pl
from jax.experimental.pallas import tpu as pltpu
from jax.sharding import PartitionSpec as P

BS = 128
BAND = 7
SLOTS = 15
ROWS = 8
NBLOCKS = 1024
DEVICES = 128
GRID = 128
SPAN = ROWS * BS
GROUP = 32
RING = 4
ATOMS_DEV = 512
ATOMS_HERE = GROUP * ATOMS_DEV

COUPLE = 0.5
DENSITY_SCALE = 0.05
ROOT = math.sqrt(math.log2(math.e) / 8.0)

MESH = pl.DeviceIdType.MESH
F32 = jnp.float32
BF16 = jnp.bfloat16


def dot(a, b):
    return jnp.dot(a, b, preferred_element_type=F32)


def dot_nt(a, b):
    return lax.dot_general(a, b, (((1,), (1,)), ((), ())), preferred_element_type=F32)


def bell(points, centre):
    offset = points - centre
    return jnp.exp2(-(offset * offset))


def kernel(
    density, mask, slabs, cells, positions, charges, new_density, energies,
    dens, left, right, s_next, s_prev, pu_out, pd_out, pu_in, pd_in,
    atoms, diff, diff_in, tab_y, tab_z, lhs, pot_acc, pot_out, pot_in, rho, e_out, e_in,
    dens_sem, out_sem, early_sem, diff_sem, gather_sem, halo_send, halo_recv, part_send, part_recv,
    pot_send, pot_recv, rho_send, rho_recv, en_send, en_recv,
):
    g, r, c = lax.axis_index("grp"), lax.axis_index("row"), lax.axis_index("col")
    me = (g * 8 + r) * 4 + c
    half, z = r // 4, r % 4
    mine = (g * 2 + half) * 4 + c

    def coords(index):
        return (index // 32, (index // 4) % 8, index % 4)

    after = coords((me + 1) % DEVICES)
    before = coords((me + DEVICES - 1) % DEVICES)

    def place(slot):
        return (slot // 8, ((slot // 4) % 2) * 4 + z, slot % 4)

    def peer(k):
        slot = (mine + k) % GROUP
        return slot, place(slot)

    def ring(k):
        return (g, half * 4 + (z + k) % RING, c)

    loads = [
        pltpu.make_async_copy(density.at[i], dens.at[i], dens_sem.at[i]) for i in range(ROWS)
    ]
    outside_in = (7, 0, 6, 1, 5, 2, 4, 3)
    for i in outside_in:
        loads[i].start()
    for j in range(4):
        for d in range(3):
            atoms[mine, pl.ds(4 * d + j, 1), :] = positions[d:d + 1, j * BS:(j + 1) * BS]
        atoms[mine, pl.ds(12 + j, 1), :] = charges[j:j + 1, :]

    barrier = pltpu.get_barrier_semaphore()

    @pl.loop(1, GROUP)
    def _(k):
        pl.semaphore_signal(barrier, inc=1, device_id=peer(k)[1], device_id_type=MESH)

    for k in range(1, RING):
        pl.semaphore_signal(barrier, inc=1, device_id=ring(k), device_id_type=MESH)
    pl.semaphore_signal(barrier, inc=1, device_id=after, device_id_type=MESH)
    pl.semaphore_signal(barrier, inc=1, device_id=before, device_id_type=MESH)
    pl.semaphore_wait(barrier, GROUP - 1 + RING - 1 + 2)

    @pl.loop(1, GROUP)
    def _(k):
        pltpu.make_async_remote_copy(
            atoms.at[mine], atoms.at[mine], gather_sem.at[0], gather_sem.at[1],
            device_id=peer(k)[1], device_id_type=MESH,
        ).start()

    zero = jnp.zeros((BS, BS), BF16)
    for a in range(0, ROWS, 2):
        for i, j in ((a, a), (a, a + 1), (a + 1, a), (a + 1, a + 1)):
            if j >= i:
                left[i * BS:(i + 1) * BS, 2 * SPAN + j * BS:2 * SPAN + (j + 1) * BS] = zero
                right[i * BS:(i + 1) * BS, j * BS:(j + 1) * BS] = zero
            if j <= i:
                left[i * BS:(i + 1) * BS, j * BS:(j + 1) * BS] = zero
                right[2 * SPAN + i * BS:2 * SPAN + (i + 1) * BS, j * BS:(j + 1) * BS] = zero

    def valid(i, s):
        column = me * ROWS + (i + s - BAND)
        inside = jnp.logical_and(column >= 0, column < NBLOCKS)
        return (mask[i, s] * inside.astype(jnp.int32)).astype(F32)

    to_next, to_prev = {}, {}
    for i in outside_in:
        loads[i].wait()
        for s in range(SLOTS):
            k = i + s + 1
            block = (dens[i, s].astype(F32) * valid(i, s)).astype(BF16)
            left[i * BS:(i + 1) * BS, k * BS:(k + 1) * BS] = block
            if ROWS <= k < 2 * ROWS:
                right[SPAN + i * BS:SPAN + (i + 1) * BS, (k - ROWS) * BS:(k - ROWS + 1) * BS] = block
        here = pl.ds(i * BS, BS)
        if i > 0:
            copy = pltpu.make_async_remote_copy(
                left.at[here, pl.ds(2 * SPAN, i * BS)], right.at[here, pl.ds(0, i * BS)],
                halo_send.at[0, i], halo_recv.at[0, i], device_id=after, device_id_type=MESH,
            )
            copy.start()
            to_next[i] = copy
        if i < ROWS - 1:
            there = pl.ds((i + 1) * BS, (ROWS - 1 - i) * BS)
            copy = pltpu.make_async_remote_copy(
                left.at[here, there], right.at[pl.ds(2 * SPAN + i * BS, BS), there],
                halo_send.at[1, i], halo_recv.at[1, i], device_id=before, device_id_type=MESH,
            )
            copy.start()
            to_prev[i] = copy

    others = atoms.at[pl.ds(0, GROUP - 1)]
    pltpu.make_async_copy(others, others, gather_sem.at[0]).wait()
    pltpu.make_async_copy(others, others, gather_sem.at[1]).wait()

    points = lax.broadcasted_iota(jnp.int32, (GRID, BS), 0).astype(F32) * ROOT
    first = me - 4 * z
    planes = [slabs[first + 4 * p].astype(F32) * ROOT for p in range(RING)]
    pot_acc[...] = jnp.zeros_like(pot_acc)

    def tables(slot):
        ys, ws = [], []
        for j in range(4):
            at = pl.ds(pl.multiple_of(slot * ATOMS_DEV + j * BS, BS), BS)
            centre = [atoms[slot, pl.ds(4 * d + j, 1), :] * (GRID * ROOT) for d in range(3)]
            charge = atoms[slot, pl.ds(12 + j, 1), :]
            along_y = bell(points, centre[1])
            high = along_y.astype(BF16)
            low = (along_y - high.astype(F32)).astype(BF16)
            tab_y[0:GRID, at] = high
            tab_y[GRID:2 * GRID, at] = low
            ys.append(jnp.concatenate([high, low], axis=0))
            along_z = bell(points, centre[2])
            tab_z[:, at] = along_z
            ws.append(jnp.concatenate([
                (along_z * (bell(planes[p], centre[0]) * charge)).astype(BF16) for p in range(RING)
            ], axis=0))
        return jnp.concatenate(ws, axis=1), jnp.concatenate(ys, axis=1)

    def partial_potential(start, stop):
        @pl.loop(start, stop)
        def _(t):
            ones = tables(2 * t)
            twos = tables(2 * t + 1)
            pot_acc[...] += dot_nt(*ones) + dot_nt(*twos)

    parts = []

    def corners(rows_next, rows_prev):
        for i in rows_next:
            to_next[i].wait()
            here, there = pl.ds(i * BS, BS), pl.ds(0, i * BS)
            pu_out[here, there] = dot(
                right[i * BS:(i + 1) * BS, 0:i * BS], right[SPAN:SPAN + i * BS, 0:i * BS]
            ).astype(BF16)
            copy = pltpu.make_async_remote_copy(
                pu_out.at[here, there], pu_in.at[here, there],
                part_send.at[0, i], part_recv.at[0, i], device_id=before, device_id_type=MESH,
            )
            copy.start()
            parts.append(copy)
        for i in rows_prev:
            to_prev[i].wait()
            start = (i + 1) * BS
            here, there = pl.ds(i * BS, BS), pl.ds(start, SPAN - start)
            pd_out[here, there] = dot(
                right[2 * SPAN + i * BS:2 * SPAN + (i + 1) * BS, start:SPAN],
                right[SPAN + start:2 * SPAN, start:SPAN],
            ).astype(BF16)
            copy = pltpu.make_async_remote_copy(
                pd_out.at[here, there], pd_in.at[here, there],
                part_send.at[1, i], part_recv.at[1, i], device_id=after, device_id_type=MESH,
            )
            copy.start()
            parts.append(copy)

    partial_potential(0, GROUP // 4)
    corners((7, 6), (0, 1))
    partial_potential(GROUP // 4, GROUP // 2)

    for p in range(RING):
        part = pot_acc[p * GRID:(p + 1) * GRID, 0:GRID] + pot_acc[p * GRID:(p + 1) * GRID, GRID:2 * GRID]
        pot_out[p] = part
    pot_copies = []
    for k in range(1, RING):
        target = (z + k) % RING
        copy = pltpu.make_async_remote_copy(
            pot_out.at[target], pot_in.at[k], pot_send.at[k], pot_recv.at[k],
            device_id=ring(k), device_id_type=MESH,
        )
        copy.start()
        pot_copies.append(copy)
    corners((5, 4, 3, 2, 1), (2, 3, 4, 5, 6))
    potential = pot_out[z]
    for k, copy in zip(range(1, RING), pot_copies):
        copy.wait()
        potential = potential + pot_in[k]

    high = potential.astype(BF16)
    both = jnp.concatenate([high, (potential - high.astype(F32)).astype(BF16)], axis=1)
    cell_y = lax.shift_right_logical(cells[...], 7)
    cell_z = jnp.bitwise_and(cells[...], GRID - 1)
    height = lax.broadcasted_iota(jnp.int32, (GRID, BS), 0)
    eye = (height == lax.broadcasted_iota(jnp.int32, (GRID, BS), 1)).astype(F32)

    def hot(cell, i):
        return (height == cell[i:i + 1, :]).astype(F32)

    for i in range(ROWS):
        hot_y = hot(cell_y, i).astype(BF16)
        rows = dot(both, jnp.concatenate([hot_y, hot_y], axis=0))
        shift = COUPLE * jnp.sum(rows * hot(cell_z, i), axis=0, keepdims=True)
        block = ((dens[i, BAND].astype(F32) - shift * eye) * valid(i, BAND)).astype(BF16)
        plain = right[SPAN + i * BS:SPAN + (i + 1) * BS, i * BS:(i + 1) * BS].astype(F32)
        diff[i:i + 1, :] = jnp.sum((block.astype(F32) - plain) * eye, axis=0, keepdims=True)
        left[i * BS:(i + 1) * BS, SPAN + i * BS:SPAN + (i + 1) * BS] = block
        right[SPAN + i * BS:SPAN + (i + 1) * BS, i * BS:(i + 1) * BS] = block

    for k, target in ((0, after), (1, before)):
        copy = pltpu.make_async_remote_copy(
            diff, diff_in.at[k], diff_sem.at[0, k], diff_sem.at[1, k],
            device_id=target, device_id_type=MESH,
        )
        copy.start()
        parts.append(copy)

    def middle(a, b):
        first, last = max(a, b) + 1, min(a, b) + 16
        window = slice(first * BS, (last + 1) * BS)
        total = dot(left[a * BS:(a + 2) * BS, window], right[window, b * BS:(b + 2) * BS])
        for i in (a, a + 1):
            for j in (b, b + 1):
                s = j - i + BAND
                held = left[i * BS:(i + 1) * BS, SPAN + j * BS:SPAN + (j + 1) * BS].astype(F32)
                square = total[(i - a) * BS:(i - a + 1) * BS, (j - b) * BS:(j - b + 1) * BS]
                dens[i, s] = ((2.0 * held - square) * valid(i, s)).astype(BF16)

    for a in range(0, ROWS, 2):
        middle(a, a)

    grid_here = jnp.zeros((GRID, GRID), F32)
    for i in range(ROWS):
        diagonal = jnp.sum(dens[i, BAND].astype(F32) * eye, axis=0, keepdims=True)
        spread = (hot(cell_z, i) * diagonal).astype(BF16)
        grid_here = grid_here + dot_nt(spread, hot(cell_y, i).astype(BF16))
    rho[0] = grid_here.astype(BF16)
    rho_copies = []
    for k in range(1, RING):
        copy = pltpu.make_async_remote_copy(
            rho.at[0], rho.at[k], rho_send.at[k], rho_recv.at[k],
            device_id=ring(k), device_id_type=MESH,
        )
        copy.start()
        rho_copies.append(copy)

    for a in range(0, ROWS, 2):
        for b in range(0, ROWS, 2):
            if a != b:
                middle(a, b)
    for b in range(0, ROWS, 2):
        columns = slice(b * BS, (b + 2) * BS)
        rows = slice((b + 1) * BS, SPAN)
        s_next[rows, columns] = dot(
            left[rows, SPAN + b * BS:2 * SPAN],
            left[b * BS:SPAN, 2 * SPAN + b * BS:2 * SPAN + (b + 2) * BS],
        )
        rows = slice(0, (b + 1) * BS)
        s_prev[rows, columns] = dot(
            left[rows, SPAN:SPAN + (b + 2) * BS], left[0:(b + 2) * BS, b * BS:(b + 2) * BS]
        )

    early = [
        pltpu.make_async_copy(
            dens.at[i, pl.ds(BAND - i, ROWS)], new_density.at[i, pl.ds(BAND - i, ROWS)], early_sem.at[i]
        )
        for i in range(ROWS)
    ]
    for copy in early:
        copy.start()
    for copy in rho_copies:
        copy.wait()

    order = [(z - k + RING) % RING for k in range(RING)]
    mine_planes = [slabs[first + 4 * order[k]].astype(F32) * ROOT for k in range(RING)]
    weights = jnp.concatenate([rho[k] for k in range(RING)], axis=0)
    lhs[:, 0:GRID] = weights
    lhs[:, GRID:2 * GRID] = weights

    @pl.loop(0, GROUP)
    def _(k):
        slot = (mine + 1 + k) % GROUP
        base = pl.multiple_of(slot * ATOMS_DEV, ATOMS_DEV)
        inner = dot(lhs[:, 0:2 * GRID], tab_y[:, pl.ds(base, ATOMS_DEV)])
        for j in range(4):
            at = pl.ds(base + j * BS, BS)
            centre = atoms[slot, pl.ds(j, 1), :] * (GRID * ROOT)
            along_z = tab_z[:, at]
            total = jnp.zeros((1, BS), F32)
            for p in range(RING):
                piece = inner[p * GRID:(p + 1) * GRID, j * BS:(j + 1) * BS]
                total += bell(mine_planes[p], centre) * jnp.sum(piece * along_z, axis=0, keepdims=True)
            e_out[slot, pl.ds(j, 1), :] = total

        @pl.when(k < GROUP - 1)
        def _():
            pltpu.make_async_remote_copy(
                e_out.at[slot], e_in.at[mine], en_send, en_recv,
                device_id=place(slot), device_id_type=MESH,
            ).start()

    e_in[mine] = e_out[mine]

    for copy in parts:
        copy.wait()
    late = []
    for i in range(ROWS):
        here = slice(i * BS, (i + 1) * BS)
        for j in range(ROWS):
            there = slice(j * BS, (j + 1) * BS)
            if j < i:
                s = j - i + SLOTS
                held = left[here, 2 * SPAN + j * BS:2 * SPAN + (j + 1) * BS].astype(F32)
                square = s_next[here, there] + pu_in[here, there].astype(F32)
                dens[i, s] = ((held * (2.0 - diff_in[1, j:j + 1, :]) - square) * valid(i, s)).astype(BF16)
            if j > i:
                s = j - i - 1
                held = left[here, there].astype(F32)
                square = s_prev[here, there] + pd_in[here, there].astype(F32)
                dens[i, s] = ((held * (2.0 - diff_in[0, j:j + 1, :]) - square) * valid(i, s)).astype(BF16)
        for k, (start, size) in enumerate(((0, BAND - i), (SLOTS - i, i))):
            if size:
                copy = pltpu.make_async_copy(
                    dens.at[i, pl.ds(start, size)], new_density.at[i, pl.ds(start, size)], out_sem.at[k, i]
                )
                copy.start()
                late.append(copy)

    others = e_out.at[pl.ds(0, GROUP - 1)]
    pltpu.make_async_copy(others, others, en_send).wait()
    pltpu.make_async_copy(others, others, en_recv).wait()
    energies[...] = jnp.sum(e_in[...], axis=0) * DENSITY_SCALE * atoms[mine, pl.ds(12, 4), :]
    for copy in early + late:
        copy.wait()


def on_device(density, block_mask, orbital_cell, slab_of_device, positions, charges):
    dma = pltpu.SemaphoreType.DMA
    new_density, energies = pl.pallas_call(
        kernel,
        out_shape=(
            jax.ShapeDtypeStruct((ROWS, SLOTS, BS, BS), BF16),
            jax.ShapeDtypeStruct((4, BS), F32),
        ),
        in_specs=[
            pl.BlockSpec(memory_space=pl.ANY),
            pl.BlockSpec(memory_space=pltpu.SMEM),
            pl.BlockSpec(memory_space=pltpu.SMEM),
            pl.BlockSpec(memory_space=pltpu.VMEM),
            pl.BlockSpec(memory_space=pltpu.VMEM),
            pl.BlockSpec(memory_space=pltpu.VMEM),
        ],
        out_specs=(pl.BlockSpec(memory_space=pl.ANY), pl.BlockSpec(memory_space=pltpu.VMEM)),
        scratch_shapes=[
            pltpu.VMEM((ROWS, SLOTS, BS, BS), BF16),
            pltpu.VMEM((SPAN, 3 * SPAN), BF16),
            pltpu.VMEM((3 * SPAN, SPAN), BF16),
            pltpu.VMEM((SPAN, SPAN), F32),
            pltpu.VMEM((SPAN, SPAN), F32),
            pltpu.VMEM((SPAN, SPAN), BF16),
            pltpu.VMEM((SPAN, SPAN), BF16),
            pltpu.VMEM((SPAN, SPAN), BF16),
            pltpu.VMEM((SPAN, SPAN), BF16),
            pltpu.VMEM((GROUP, 16, BS), F32),
            pltpu.VMEM((ROWS, BS), F32),
            pltpu.VMEM((2, ROWS, BS), F32),
            pltpu.VMEM((2 * GRID, ATOMS_HERE), BF16),
            pltpu.VMEM((GRID, ATOMS_HERE), F32),
            pltpu.VMEM((RING * GRID, ATOMS_DEV), BF16),
            pltpu.VMEM((RING * GRID, 2 * GRID), F32),
            pltpu.VMEM((RING, GRID, GRID), F32),
            pltpu.VMEM((RING, GRID, GRID), F32),
            pltpu.VMEM((RING, GRID, GRID), BF16),
            pltpu.VMEM((GROUP, 4, BS), F32),
            pltpu.VMEM((GROUP, 4, BS), F32),
            dma((ROWS,)),
            dma((2, ROWS)),
            dma((ROWS,)),
            dma((2, 2)),
            dma((2,)),
            dma((2, ROWS)),
            dma((2, ROWS)),
            dma((2, ROWS)),
            dma((2, ROWS)),
            dma((RING,)),
            dma((RING,)),
            dma((RING,)),
            dma((RING,)),
            dma,
            dma,
        ],
        compiler_params=pltpu.CompilerParams(
            collective_id=0, has_side_effects=True, vmem_limit_bytes=60 * 1024 * 1024
        ),
        cost_estimate=pl.CostEstimate(flops=10**10, bytes_accessed=10**7, transcendentals=4 * 10**6),
        name="purify",
    )(density, block_mask, slab_of_device, orbital_cell.reshape(ROWS, BS), positions, charges.reshape(4, BS))
    return new_density, energies.reshape(ATOMS_DEV)


def solution(mesh):
    in_specs = (
        P(("grp", "row", "col"), None, None, None),
        P(("grp", "row", "col"), None),
        P(("grp", "row", "col")),
        P(),
        P(None, ("grp", "row", "col")),
        P(("grp", "row", "col")),
    )
    out_specs = (P(("grp", "row", "col"), None, None, None), P(("grp", "row", "col")))
    return jax.shard_map(
        on_device, mesh=mesh, in_specs=in_specs, out_specs=out_specs, check_vma=False
    )
```

```python
import functools
import math

import jax
import jax.numpy as jnp
from jax import lax
from jax.experimental import pallas as pl
from jax.experimental.pallas import tpu as pltpu
from jax.sharding import PartitionSpec as P

BS = 128
BAND = 7
SLOTS = 15
ROWS = 8
NBLOCKS = 1024
DEVICES = 128
GRID = 128
SPAN = ROWS * BS
GROUP = 32
RING = 4
ATOMS_DEV = 512
ATOMS_HERE = GROUP * ATOMS_DEV

COUPLE = 0.5
DENSITY_SCALE = 0.05
ROOT = math.sqrt(math.log2(math.e) / 8.0)

MESH = pl.DeviceIdType.MESH
F32 = jnp.float32
BF16 = jnp.bfloat16


def dot(a, b):
    return jnp.dot(a, b, preferred_element_type=F32)


def dot_nt(a, b):
    return lax.dot_general(a, b, (((1,), (1,)), ((), ())), preferred_element_type=F32)


def bell(points, centre):
    offset = points - centre
    return jnp.exp2(-(offset * offset))


def kernel(
    density, mask, slabs, cells, positions, charges, dens, energies,
    left, right, outer, pu_out, pd_out, pu_in, pd_in,
    atoms, diff, diff_in, tab_y, tab_z, lhs, pot_acc, pot_out, pot_in, rho, e_out, e_in,
    dens_sem, diff_sem, gather_sem, halo_send, halo_recv, part_send, part_recv,
    pot_send, pot_recv, rho_send, rho_recv, en_send, en_recv,
):
    g, r, c = lax.axis_index("grp"), lax.axis_index("row"), lax.axis_index("col")
    me = (g * 8 + r) * 4 + c
    half, z = r // 4, r % 4
    mine = (g * 2 + half) * 4 + c

    def coords(index):
        return (index // 32, (index // 4) % 8, index % 4)

    after = coords((me + 1) % DEVICES)
    before = coords((me + DEVICES - 1) % DEVICES)

    def place(slot):
        return (slot // 8, ((slot // 4) % 2) * 4 + z, slot % 4)

    def peer(k):
        slot = (mine + k) % GROUP
        return slot, place(slot)

    def ring(k):
        return (g, half * 4 + (z + k) % RING, c)

    loads = [
        pltpu.make_async_copy(density.at[i], dens.at[i], dens_sem.at[i]) for i in range(ROWS)
    ]
    outside_in = (7, 0, 6, 1, 5, 2, 4, 3)
    for i in outside_in:
        loads[i].start()
    for j in range(4):
        for d in range(3):
            atoms[mine, pl.ds(4 * d + j, 1), :] = positions[d:d + 1, j * BS:(j + 1) * BS]
        atoms[mine, pl.ds(12 + j, 1), :] = charges[j:j + 1, :]

    barrier = pltpu.get_barrier_semaphore()

    @pl.loop(1, GROUP)
    def _(k):
        pl.semaphore_signal(barrier, inc=1, device_id=peer(k)[1], device_id_type=MESH)

    for k in range(1, RING):
        pl.semaphore_signal(barrier, inc=1, device_id=ring(k), device_id_type=MESH)
    pl.semaphore_signal(barrier, inc=1, device_id=after, device_id_type=MESH)
    pl.semaphore_signal(barrier, inc=1, device_id=before, device_id_type=MESH)
    pl.semaphore_wait(barrier, GROUP - 1 + RING - 1 + 2)

    @pl.loop(1, GROUP)
    def _(k):
        pltpu.make_async_remote_copy(
            atoms.at[mine], atoms.at[mine], gather_sem.at[0], gather_sem.at[1],
            device_id=peer(k)[1], device_id_type=MESH,
        ).start()

    zero = jnp.zeros((BS, BS), BF16)
    for a in range(0, ROWS, 2):
        for i, j in ((a, a), (a, a + 1), (a + 1, a), (a + 1, a + 1)):
            if j >= i:
                left[i * BS:(i + 1) * BS, 2 * SPAN + j * BS:2 * SPAN + (j + 1) * BS] = zero
                right[i * BS:(i + 1) * BS, j * BS:(j + 1) * BS] = zero
            if j <= i:
                left[i * BS:(i + 1) * BS, j * BS:(j + 1) * BS] = zero
                right[2 * SPAN + i * BS:2 * SPAN + (i + 1) * BS, j * BS:(j + 1) * BS] = zero

    def valid(i, s):
        column = me * ROWS + (i + s - BAND)
        inside = jnp.logical_and(column >= 0, column < NBLOCKS)
        return (mask[i, s] * inside.astype(jnp.int32)).astype(F32)

    to_next, to_prev = {}, {}
    for i in outside_in:
        loads[i].wait()
        for s in range(SLOTS):
            k = i + s + 1
            block = (dens[i, s].astype(F32) * valid(i, s)).astype(BF16)
            left[i * BS:(i + 1) * BS, k * BS:(k + 1) * BS] = block
            if ROWS <= k < 2 * ROWS:
                right[SPAN + i * BS:SPAN + (i + 1) * BS, (k - ROWS) * BS:(k - ROWS + 1) * BS] = block
        here = pl.ds(i * BS, BS)
        if i > 0:
            copy = pltpu.make_async_remote_copy(
                left.at[here, pl.ds(2 * SPAN, i * BS)], right.at[here, pl.ds(0, i * BS)],
                halo_send.at[0, i], halo_recv.at[0, i], device_id=after, device_id_type=MESH,
            )
            copy.start()
            to_next[i] = copy
        if i < ROWS - 1:
            there = pl.ds((i + 1) * BS, (ROWS - 1 - i) * BS)
            copy = pltpu.make_async_remote_copy(
                left.at[here, there], right.at[pl.ds(2 * SPAN + i * BS, BS), there],
                halo_send.at[1, i], halo_recv.at[1, i], device_id=before, device_id_type=MESH,
            )
            copy.start()
            to_prev[i] = copy

    others = atoms.at[pl.ds(0, GROUP - 1)]
    pltpu.make_async_copy(others, others, gather_sem.at[0]).wait()
    pltpu.make_async_copy(others, others, gather_sem.at[1]).wait()

    points = lax.broadcasted_iota(jnp.int32, (GRID, BS), 0).astype(F32) * ROOT
    first = me - 4 * z
    planes = [slabs[first + 4 * p].astype(F32) * ROOT for p in range(RING)]
    pot_acc[...] = jnp.zeros_like(pot_acc)

    def tables(slot):
        ys, ws = [], []
        for j in range(4):
            at = pl.ds(pl.multiple_of(slot * ATOMS_DEV + j * BS, BS), BS)
            centre = [atoms[slot, pl.ds(4 * d + j, 1), :] * (GRID * ROOT) for d in range(3)]
            charge = atoms[slot, pl.ds(12 + j, 1), :]
            along_y = bell(points, centre[1])
            high = along_y.astype(BF16)
            low = (along_y - high.astype(F32)).astype(BF16)
            tab_y[0:GRID, at] = high
            tab_y[GRID:2 * GRID, at] = low
            ys.append(jnp.concatenate([high, low], axis=0))
            along_z = bell(points, centre[2])
            tab_z[:, at] = along_z
            ws.append(jnp.concatenate([
                (along_z * (bell(planes[p], centre[0]) * charge)).astype(BF16) for p in range(RING)
            ], axis=0))
        return jnp.concatenate(ws, axis=1), jnp.concatenate(ys, axis=1)

    def partial_potential(start, stop):
        @pl.loop(start, stop)
        def _(t):
            ones = tables(2 * t)
            twos = tables(2 * t + 1)
            pot_acc[...] += dot_nt(*ones) + dot_nt(*twos)

    pairs = []

    def corners(n):
        i = BAND - n
        to_next[i].wait()
        here, there = pl.ds(i * BS, BS), pl.ds(0, i * BS)
        pu_out[here, there] = dot(
            right[i * BS:(i + 1) * BS, 0:i * BS], right[SPAN:SPAN + i * BS, 0:i * BS]
        ).astype(BF16)
        up = pltpu.make_async_remote_copy(
            pu_out.at[here, there], pu_in.at[here, there],
            part_send.at[0, i], part_recv.at[0, i], device_id=before, device_id_type=MESH,
        )
        to_prev[n].wait()
        start = (n + 1) * BS
        here, there = pl.ds(n * BS, BS), pl.ds(start, SPAN - start)
        pd_out[here, there] = dot(
            right[2 * SPAN + n * BS:2 * SPAN + (n + 1) * BS, start:SPAN],
            right[SPAN + start:2 * SPAN, start:SPAN],
        ).astype(BF16)
        down = pltpu.make_async_remote_copy(
            pd_out.at[here, there], pd_in.at[here, there],
            part_send.at[1, n], part_recv.at[1, n], device_id=after, device_id_type=MESH,
        )
        pairs.append((up, down))

    def start_pair(n):
        for copy in pairs[n]:
            copy.start()

    def sent_pair(n):
        for copy in pairs[n]:
            copy.wait_send()

    partial_potential(0, GROUP // 2)

    for p in range(RING):
        part = pot_acc[p * GRID:(p + 1) * GRID, 0:GRID] + pot_acc[p * GRID:(p + 1) * GRID, GRID:2 * GRID]
        pot_out[p] = part
    pot_copies = []
    for k in range(1, RING):
        target = (z + k) % RING
        copy = pltpu.make_async_remote_copy(
            pot_out.at[target], pot_in.at[k], pot_send.at[k], pot_recv.at[k],
            device_id=ring(k), device_id_type=MESH,
        )
        copy.start()
        pot_copies.append(copy)
    corners(0)
    start_pair(0)
    for n in range(1, BAND):
        corners(n)
    potential = pot_out[z]
    for k, copy in zip(range(1, RING), pot_copies):
        copy.wait()
        potential = potential + pot_in[k]

    high = potential.astype(BF16)
    both = jnp.concatenate([high, (potential - high.astype(F32)).astype(BF16)], axis=1)
    cell_y = lax.shift_right_logical(cells[...], 7)
    cell_z = jnp.bitwise_and(cells[...], GRID - 1)
    height = lax.broadcasted_iota(jnp.int32, (GRID, BS), 0)
    eye = (height == lax.broadcasted_iota(jnp.int32, (GRID, BS), 1)).astype(F32)

    def hot(cell, i):
        return (height == cell[i:i + 1, :]).astype(F32)

    for i in range(ROWS):
        hot_y = hot(cell_y, i).astype(BF16)
        rows = dot(both, jnp.concatenate([hot_y, hot_y], axis=0))
        shift = COUPLE * jnp.sum(rows * hot(cell_z, i), axis=0, keepdims=True)
        block = ((dens[i, BAND].astype(F32) - shift * eye) * valid(i, BAND)).astype(BF16)
        plain = right[SPAN + i * BS:SPAN + (i + 1) * BS, i * BS:(i + 1) * BS].astype(F32)
        diff[i:i + 1, :] = jnp.sum((block.astype(F32) - plain) * eye, axis=0, keepdims=True)
        left[i * BS:(i + 1) * BS, SPAN + i * BS:SPAN + (i + 1) * BS] = block
        right[SPAN + i * BS:SPAN + (i + 1) * BS, i * BS:(i + 1) * BS] = block

    diff_copies = []
    for k, target in ((0, after), (1, before)):
        copy = pltpu.make_async_remote_copy(
            diff, diff_in.at[k], diff_sem.at[0, k], diff_sem.at[1, k],
            device_id=target, device_id_type=MESH,
        )
        copy.start()
        diff_copies.append(copy)

    def middle(a, b):
        first, last = max(a, b) + 1, min(a, b) + 16
        window = slice(first * BS, (last + 1) * BS)
        total = dot(left[a * BS:(a + 2) * BS, window], right[window, b * BS:(b + 2) * BS])
        for i in (a, a + 1):
            for j in (b, b + 1):
                s = j - i + BAND
                held = left[i * BS:(i + 1) * BS, SPAN + j * BS:SPAN + (j + 1) * BS].astype(F32)
                square = total[(i - a) * BS:(i - a + 1) * BS, (j - b) * BS:(j - b + 1) * BS]
                dens[i, s] = ((2.0 * held - square) * valid(i, s)).astype(BF16)

    for a in range(0, ROWS, 2):
        middle(a, a)

    grid_here = jnp.zeros((GRID, GRID), F32)
    for i in range(ROWS):
        diagonal = jnp.sum(dens[i, BAND].astype(F32) * eye, axis=0, keepdims=True)
        spread = (hot(cell_z, i) * diagonal).astype(BF16)
        grid_here = grid_here + dot_nt(spread, hot(cell_y, i).astype(BF16))
    rho[0] = grid_here.astype(BF16)
    rho_copies = []
    for k in range(1, RING):
        copy = pltpu.make_async_remote_copy(
            rho.at[0], rho.at[k], rho_send.at[k], rho_recv.at[k],
            device_id=ring(k), device_id_type=MESH,
        )
        copy.start()
        rho_copies.append(copy)
    start_pair(1)
    start_pair(2)

    for a in range(0, ROWS, 2):
        for b in range(0, ROWS, 2):
            if a != b:
                middle(a, b)
    for b in range(0, ROWS, 2):
        columns = slice(b * BS, (b + 2) * BS)
        rows = slice((b + 1) * BS, SPAN)
        outer[rows, columns] = dot(
            left[rows, SPAN + b * BS:2 * SPAN],
            left[b * BS:SPAN, 2 * SPAN + b * BS:2 * SPAN + (b + 2) * BS],
        )
        rows = slice(0, (b + 1) * BS)
        outer[rows, columns] = dot(
            left[rows, SPAN:SPAN + (b + 2) * BS], left[0:(b + 2) * BS, b * BS:(b + 2) * BS]
        )

    for copy in rho_copies:
        copy.wait()

    order = [(z - k + RING) % RING for k in range(RING)]
    mine_planes = [slabs[first + 4 * order[k]].astype(F32) * ROOT for k in range(RING)]
    weights = jnp.concatenate([rho[k] for k in range(RING)], axis=0)
    lhs[:, 0:GRID] = weights
    lhs[:, GRID:2 * GRID] = weights

    @pl.loop(0, GROUP)
    def _(k):
        slot = (mine + 1 + k) % GROUP
        base = pl.multiple_of(slot * ATOMS_DEV, ATOMS_DEV)
        inner = dot(lhs[:, 0:2 * GRID], tab_y[:, pl.ds(base, ATOMS_DEV)])
        for j in range(4):
            at = pl.ds(base + j * BS, BS)
            centre = atoms[slot, pl.ds(j, 1), :] * (GRID * ROOT)
            along_z = tab_z[:, at]
            total = jnp.zeros((1, BS), F32)
            for p in range(RING):
                piece = inner[p * GRID:(p + 1) * GRID, j * BS:(j + 1) * BS]
                total += bell(mine_planes[p], centre) * jnp.sum(piece * along_z, axis=0, keepdims=True)
            e_out[slot, pl.ds(j, 1), :] = total

        for when, n in ((4, 3), (12, 4), (20, 5), (26, 6)):
            @pl.when(k == when)
            def _(n=n):
                sent_pair(n - 2)
                start_pair(n)

        @pl.when(k < GROUP - 1)
        def _():
            pltpu.make_async_remote_copy(
                e_out.at[slot], e_in.at[mine], en_send, en_recv,
                device_id=place(slot), device_id_type=MESH,
            ).start()

    e_in[mine] = e_out[mine]

    for copy in diff_copies:
        copy.wait()
    for n in range(BAND):
        up, down = pairs[n]
        if n == 0 or n > 4:
            up.wait_send()
            down.wait_send()
        up.wait_recv()
        i = BAND - n
        here = slice(i * BS, (i + 1) * BS)
        for j in range(i):
            there = slice(j * BS, (j + 1) * BS)
            s = j - i + SLOTS
            held = left[here, 2 * SPAN + j * BS:2 * SPAN + (j + 1) * BS].astype(F32)
            square = outer[here, there] + pu_in[here, there].astype(F32)
            dens[i, s] = ((held * (2.0 - diff_in[1, j:j + 1, :]) - square) * valid(i, s)).astype(BF16)
        down.wait_recv()
        here = slice(n * BS, (n + 1) * BS)
        for j in range(n + 1, ROWS):
            there = slice(j * BS, (j + 1) * BS)
            s = j - n - 1
            held = left[here, there].astype(F32)
            square = outer[here, there] + pd_in[here, there].astype(F32)
            dens[n, s] = ((held * (2.0 - diff_in[0, j:j + 1, :]) - square) * valid(n, s)).astype(BF16)

    others = e_out.at[pl.ds(0, GROUP - 1)]
    pltpu.make_async_copy(others, others, en_send).wait()
    pltpu.make_async_copy(others, others, en_recv).wait()
    energies[...] = jnp.sum(e_in[...], axis=0) * DENSITY_SCALE * atoms[mine, pl.ds(12, 4), :]


def on_device(density, block_mask, orbital_cell, slab_of_device, positions, charges):
    dma = pltpu.SemaphoreType.DMA
    new_density, energies = pl.pallas_call(
        kernel,
        out_shape=(
            pltpu.VMEM((ROWS, SLOTS, BS, BS), BF16),
            pltpu.VMEM((4, BS), F32),
        ),
        in_specs=[
            pl.BlockSpec(memory_space=pl.ANY),
            pl.BlockSpec(memory_space=pltpu.SMEM),
            pl.BlockSpec(memory_space=pltpu.SMEM),
            pl.BlockSpec(memory_space=pltpu.VMEM),
            pl.BlockSpec(memory_space=pltpu.VMEM),
            pl.BlockSpec(memory_space=pltpu.VMEM),
        ],
        out_specs=(pl.BlockSpec(memory_space=pltpu.VMEM), pl.BlockSpec(memory_space=pltpu.VMEM)),
        scratch_shapes=[
            pltpu.VMEM((SPAN, 3 * SPAN), BF16),
            pltpu.VMEM((3 * SPAN, SPAN), BF16),
            pltpu.VMEM((SPAN, SPAN), F32),
            pltpu.VMEM((SPAN, SPAN), BF16),
            pltpu.VMEM((SPAN, SPAN), BF16),
            pltpu.VMEM((SPAN, SPAN), BF16),
            pltpu.VMEM((SPAN, SPAN), BF16),
            pltpu.VMEM((GROUP, 16, BS), F32),
            pltpu.VMEM((ROWS, BS), F32),
            pltpu.VMEM((2, ROWS, BS), F32),
            pltpu.VMEM((2 * GRID, ATOMS_HERE), BF16),
            pltpu.VMEM((GRID, ATOMS_HERE), F32),
            pltpu.VMEM((RING * GRID, ATOMS_DEV), BF16),
            pltpu.VMEM((RING * GRID, 2 * GRID), F32),
            pltpu.VMEM((RING, GRID, GRID), F32),
            pltpu.VMEM((RING, GRID, GRID), F32),
            pltpu.VMEM((RING, GRID, GRID), BF16),
            pltpu.VMEM((GROUP, 4, BS), F32),
            pltpu.VMEM((GROUP, 4, BS), F32),
            dma((ROWS,)),
            dma((2, 2)),
            dma((2,)),
            dma((2, ROWS)),
            dma((2, ROWS)),
            dma((2, ROWS)),
            dma((2, ROWS)),
            dma((RING,)),
            dma((RING,)),
            dma((RING,)),
            dma((RING,)),
            dma,
            dma,
        ],
        compiler_params=pltpu.CompilerParams(
            collective_id=0, has_side_effects=True, vmem_limit_bytes=52 * 1024 * 1024
        ),
        cost_estimate=pl.CostEstimate(flops=10**10, bytes_accessed=10**7, transcendentals=4 * 10**6),
        name="purify",
    )(density, block_mask, slab_of_device, orbital_cell.reshape(ROWS, BS), positions, charges.reshape(4, BS))
    return new_density, energies.reshape(ATOMS_DEV)


def solution(mesh):
    in_specs = (
        P(("grp", "row", "col"), None, None, None),
        P(("grp", "row", "col"), None),
        P(("grp", "row", "col")),
        P(),
        P(None, ("grp", "row", "col")),
        P(("grp", "row", "col")),
    )
    out_specs = (P(("grp", "row", "col"), None, None, None), P(("grp", "row", "col")))
    return jax.shard_map(
        on_device, mesh=mesh, in_specs=in_specs, out_specs=out_specs, check_vma=False
    )
```

```python
import functools
import math

import jax
import jax.numpy as jnp
from jax import lax
from jax.experimental import pallas as pl
from jax.experimental.pallas import tpu as pltpu
from jax.sharding import PartitionSpec as P

BS = 128
BAND = 7
SLOTS = 15
ROWS = 8
NBLOCKS = 1024
DEVICES = 128
GRID = 128
SPAN = ROWS * BS
GROUP = 32
RING = 4
ATOMS_DEV = 512
ATOMS_HERE = GROUP * ATOMS_DEV

COUPLE = 0.5
DENSITY_SCALE = 0.05
ROOT = math.sqrt(math.log2(math.e) / 8.0)

MESH = pl.DeviceIdType.MESH
F32 = jnp.float32
BF16 = jnp.bfloat16


def dot(a, b):
    return jnp.dot(a, b, preferred_element_type=F32)


def dot_nt(a, b):
    return lax.dot_general(a, b, (((1,), (1,)), ((), ())), preferred_element_type=F32)


def bell(points, centre):
    offset = points - centre
    return jnp.exp2(-(offset * offset))


def kernel(
    density, mask, slabs, cells, positions, charges, dens, energies,
    left, right, outer, pu_out, pd_out, pu_in, pd_in,
    atoms, tab_y, tab_z, lhs, pot_acc, pot_out, pot_in, rho, e_out, e_in,
    dens_sem, gather_sem, halo_send, halo_recv, part_send, part_recv,
    pot_send, pot_recv, rho_send, rho_recv, en_send, en_recv,
):
    g, r, c = lax.axis_index("grp"), lax.axis_index("row"), lax.axis_index("col")
    me = (g * 8 + r) * 4 + c
    half, z = r // 4, r % 4
    mine = (g * 2 + half) * 4 + c

    def coords(index):
        return (index // 32, (index // 4) % 8, index % 4)

    after = coords((me + 1) % DEVICES)
    before = coords((me + DEVICES - 1) % DEVICES)

    def place(slot):
        return (slot // 8, ((slot // 4) % 2) * 4 + z, slot % 4)

    def peer(k):
        slot = (mine + k) % GROUP
        return slot, place(slot)

    def ring(k):
        return (g, half * 4 + (z + k) % RING, c)

    loads = [
        pltpu.make_async_copy(density.at[i], dens.at[i], dens_sem.at[i]) for i in range(ROWS)
    ]
    outside_in = (7, 0, 6, 1, 5, 2, 4, 3)
    for i in outside_in:
        loads[i].start()
    for j in range(4):
        for d in range(3):
            atoms[mine, pl.ds(4 * d + j, 1), :] = positions[d:d + 1, j * BS:(j + 1) * BS]
        atoms[mine, pl.ds(12 + j, 1), :] = charges[j:j + 1, :]

    barrier = pltpu.get_barrier_semaphore()

    @pl.loop(1, GROUP)
    def _(k):
        pl.semaphore_signal(barrier, inc=1, device_id=peer(k)[1], device_id_type=MESH)

    for k in range(1, RING):
        pl.semaphore_signal(barrier, inc=1, device_id=ring(k), device_id_type=MESH)
    pl.semaphore_signal(barrier, inc=1, device_id=after, device_id_type=MESH)
    pl.semaphore_signal(barrier, inc=1, device_id=before, device_id_type=MESH)
    pl.semaphore_wait(barrier, GROUP - 1 + RING - 1 + 2)

    @pl.loop(1, GROUP)
    def _(k):
        pltpu.make_async_remote_copy(
            atoms.at[mine], atoms.at[mine], gather_sem.at[0], gather_sem.at[1],
            device_id=peer(k)[1], device_id_type=MESH,
        ).start()

    zero = jnp.zeros((BS, BS), BF16)
    for a in range(0, ROWS, 2):
        for i, j in ((a, a), (a, a + 1), (a + 1, a), (a + 1, a + 1)):
            if j >= i:
                left[i * BS:(i + 1) * BS, 2 * SPAN + j * BS:2 * SPAN + (j + 1) * BS] = zero
                right[i * BS:(i + 1) * BS, j * BS:(j + 1) * BS] = zero
            if j <= i:
                left[i * BS:(i + 1) * BS, j * BS:(j + 1) * BS] = zero
                right[2 * SPAN + i * BS:2 * SPAN + (i + 1) * BS, j * BS:(j + 1) * BS] = zero

    def valid(i, s):
        column = me * ROWS + (i + s - BAND)
        inside = jnp.logical_and(column >= 0, column < NBLOCKS)
        return (mask[i, s] * inside.astype(jnp.int32)).astype(F32)

    to_next, to_prev = {}, {}
    for i in outside_in:
        loads[i].wait()
        for s in range(SLOTS):
            k = i + s + 1
            block = (dens[i, s].astype(F32) * valid(i, s)).astype(BF16)
            left[i * BS:(i + 1) * BS, k * BS:(k + 1) * BS] = block
            if ROWS <= k < 2 * ROWS:
                right[SPAN + i * BS:SPAN + (i + 1) * BS, (k - ROWS) * BS:(k - ROWS + 1) * BS] = block
        here = pl.ds(i * BS, BS)
        if i > 0:
            copy = pltpu.make_async_remote_copy(
                left.at[here, pl.ds(2 * SPAN, i * BS)], right.at[here, pl.ds(0, i * BS)],
                halo_send.at[0, i], halo_recv.at[0, i], device_id=after, device_id_type=MESH,
            )
            copy.start()
            to_next[i] = copy
        if i < ROWS - 1:
            there = pl.ds((i + 1) * BS, (ROWS - 1 - i) * BS)
            copy = pltpu.make_async_remote_copy(
                left.at[here, there], right.at[pl.ds(2 * SPAN + i * BS, BS), there],
                halo_send.at[1, i], halo_recv.at[1, i], device_id=before, device_id_type=MESH,
            )
            copy.start()
            to_prev[i] = copy

    others = atoms.at[pl.ds(0, GROUP - 1)]
    pltpu.make_async_copy(others, others, gather_sem.at[0]).wait()
    pltpu.make_async_copy(others, others, gather_sem.at[1]).wait()

    points = lax.broadcasted_iota(jnp.int32, (GRID, BS), 0).astype(F32) * ROOT
    first = me - 4 * z
    planes = [slabs[first + 4 * p].astype(F32) * ROOT for p in range(RING)]
    pot_acc[...] = jnp.zeros_like(pot_acc)

    def tables(slot):
        ys, ws = [], []
        for j in range(4):
            at = pl.ds(pl.multiple_of(slot * ATOMS_DEV + j * BS, BS), BS)
            centre = [atoms[slot, pl.ds(4 * d + j, 1), :] * (GRID * ROOT) for d in range(3)]
            charge = atoms[slot, pl.ds(12 + j, 1), :]
            along_y = bell(points, centre[1])
            high = along_y.astype(BF16)
            low = (along_y - high.astype(F32)).astype(BF16)
            tab_y[0:GRID, at] = high
            tab_y[GRID:2 * GRID, at] = low
            ys.append(jnp.concatenate([high, low], axis=0))
            along_z = bell(points, centre[2])
            tab_z[:, at] = along_z
            ws.append(jnp.concatenate([
                (along_z * (bell(planes[p], centre[0]) * charge)).astype(BF16) for p in range(RING)
            ], axis=0))
        return jnp.concatenate(ws, axis=1), jnp.concatenate(ys, axis=1)

    def partial_potential(start, stop):
        @pl.loop(start, stop)
        def _(t):
            ones = tables(2 * t)
            twos = tables(2 * t + 1)
            pot_acc[...] += dot_nt(*ones) + dot_nt(*twos)

    pairs = []

    def corners(n):
        i = BAND - n
        here, there = pl.ds(i * BS, BS), pl.ds(0, i * BS)
        pu_out[here, there] = dot(
            right[i * BS:(i + 1) * BS, 0:i * BS], right[SPAN:SPAN + i * BS, 0:i * BS]
        ).astype(BF16)
        up = pltpu.make_async_remote_copy(
            pu_out.at[here, there], pu_in.at[here, there],
            part_send.at[0, i], part_recv.at[0, i], device_id=before, device_id_type=MESH,
        )
        start = (n + 1) * BS
        here, there = pl.ds(n * BS, BS), pl.ds(start, SPAN - start)
        pd_out[here, there] = dot(
            right[2 * SPAN + n * BS:2 * SPAN + (n + 1) * BS, start:SPAN],
            right[SPAN + start:2 * SPAN, start:SPAN],
        ).astype(BF16)
        down = pltpu.make_async_remote_copy(
            pd_out.at[here, there], pd_in.at[here, there],
            part_send.at[1, n], part_recv.at[1, n], device_id=after, device_id_type=MESH,
        )
        pairs.append((up, down))

    def start_pair(n):
        for copy in pairs[n]:
            copy.start()

    def halo_pair(n):
        to_next[BAND - n].wait()
        to_prev[n].wait()

    partial_potential(0, GROUP // 2)

    for p in range(RING):
        part = pot_acc[p * GRID:(p + 1) * GRID, 0:GRID] + pot_acc[p * GRID:(p + 1) * GRID, GRID:2 * GRID]
        pot_out[p] = part
    pot_copies = []
    for k in range(1, RING):
        target = (z + k) % RING
        copy = pltpu.make_async_remote_copy(
            pot_out.at[target], pot_in.at[k], pot_send.at[k], pot_recv.at[k],
            device_id=ring(k), device_id_type=MESH,
        )
        copy.start()
        pot_copies.append(copy)
    potential = pot_out[z]
    for k, copy in zip(range(1, RING), pot_copies):
        copy.wait()
        potential = potential + pot_in[k]

    high = potential.astype(BF16)
    both = jnp.concatenate([high, (potential - high.astype(F32)).astype(BF16)], axis=1)
    cell_y = lax.shift_right_logical(cells[...], 7)
    cell_z = jnp.bitwise_and(cells[...], GRID - 1)
    height = lax.broadcasted_iota(jnp.int32, (GRID, BS), 0)
    eye = (height == lax.broadcasted_iota(jnp.int32, (GRID, BS), 1)).astype(F32)

    def hot(cell, i):
        return (height == cell[i:i + 1, :]).astype(F32)

    for i in range(ROWS):
        hot_y = hot(cell_y, i).astype(BF16)
        rows = dot(both, jnp.concatenate([hot_y, hot_y], axis=0))
        shift = COUPLE * jnp.sum(rows * hot(cell_z, i), axis=0, keepdims=True)
        block = ((dens[i, BAND].astype(F32) - shift * eye) * valid(i, BAND)).astype(BF16)
        left[i * BS:(i + 1) * BS, SPAN + i * BS:SPAN + (i + 1) * BS] = block
        right[SPAN + i * BS:SPAN + (i + 1) * BS, i * BS:(i + 1) * BS] = block

    halo_pair(0)
    corners(0)
    for n in range(1, BAND):
        halo_pair(n)
    start_pair(0)

    def middle(a, b):
        first, last = max(a, b) + 1, min(a, b) + 16
        window = slice(first * BS, (last + 1) * BS)
        total = dot(left[a * BS:(a + 2) * BS, window], right[window, b * BS:(b + 2) * BS])
        for i in (a, a + 1):
            for j in (b, b + 1):
                s = j - i + BAND
                held = left[i * BS:(i + 1) * BS, SPAN + j * BS:SPAN + (j + 1) * BS].astype(F32)
                square = total[(i - a) * BS:(i - a + 1) * BS, (j - b) * BS:(j - b + 1) * BS]
                dens[i, s] = ((2.0 * held - square) * valid(i, s)).astype(BF16)

    for a in range(0, ROWS, 2):
        middle(a, a)

    grid_here = jnp.zeros((GRID, GRID), F32)
    for i in range(ROWS):
        diagonal = jnp.sum(dens[i, BAND].astype(F32) * eye, axis=0, keepdims=True)
        spread = (hot(cell_z, i) * diagonal).astype(BF16)
        grid_here = grid_here + dot_nt(spread, hot(cell_y, i).astype(BF16))
    rho[0] = grid_here.astype(BF16)
    rho_copies = []
    for k in range(1, RING):
        copy = pltpu.make_async_remote_copy(
            rho.at[0], rho.at[k], rho_send.at[k], rho_recv.at[k],
            device_id=ring(k), device_id_type=MESH,
        )
        copy.start()
        rho_copies.append(copy)
    for n in range(1, BAND):
        corners(n)
        if n < 3:
            start_pair(n)

    for a in range(0, ROWS, 2):
        for b in range(0, ROWS, 2):
            if a != b:
                middle(a, b)
    for b in range(0, ROWS, 2):
        columns = slice(b * BS, (b + 2) * BS)
        rows = slice((b + 1) * BS, SPAN)
        outer[rows, columns] = dot(
            left[rows, SPAN + b * BS:2 * SPAN],
            left[b * BS:SPAN, 2 * SPAN + b * BS:2 * SPAN + (b + 2) * BS],
        )
        rows = slice(0, (b + 1) * BS)
        outer[rows, columns] = dot(
            left[rows, SPAN:SPAN + (b + 2) * BS], left[0:(b + 2) * BS, b * BS:(b + 2) * BS]
        )

    for copy in rho_copies:
        copy.wait()

    for n in range(3, BAND):
        start_pair(n)

    order = [(z - k + RING) % RING for k in range(RING)]
    mine_planes = [slabs[first + 4 * order[k]].astype(F32) * ROOT for k in range(RING)]
    weights = jnp.concatenate([rho[k] for k in range(RING)], axis=0)
    lhs[:, 0:GRID] = weights
    lhs[:, GRID:2 * GRID] = weights

    @pl.loop(0, GROUP)
    def _(k):
        slot = (mine + 1 + k) % GROUP
        base = pl.multiple_of(slot * ATOMS_DEV, ATOMS_DEV)
        inner = dot(lhs[:, 0:2 * GRID], tab_y[:, pl.ds(base, ATOMS_DEV)])
        for j in range(4):
            at = pl.ds(base + j * BS, BS)
            centre = atoms[slot, pl.ds(j, 1), :] * (GRID * ROOT)
            along_z = tab_z[:, at]
            total = jnp.zeros((1, BS), F32)
            for p in range(RING):
                piece = inner[p * GRID:(p + 1) * GRID, j * BS:(j + 1) * BS]
                total += bell(mine_planes[p], centre) * jnp.sum(piece * along_z, axis=0, keepdims=True)
            e_out[slot, pl.ds(j, 1), :] = total

        @pl.when(k < GROUP - 1)
        def _():
            pltpu.make_async_remote_copy(
                e_out.at[slot], e_in.at[mine], en_send, en_recv,
                device_id=place(slot), device_id_type=MESH,
            ).start()

    e_in[mine] = e_out[mine]

    for n in range(BAND):
        up, down = pairs[n]
        up.wait()
        i = BAND - n
        here = slice(i * BS, (i + 1) * BS)
        for j in range(i):
            there = slice(j * BS, (j + 1) * BS)
            s = j - i + SLOTS
            held = left[here, 2 * SPAN + j * BS:2 * SPAN + (j + 1) * BS].astype(F32)
            square = outer[here, there] + pu_in[here, there].astype(F32)
            dens[i, s] = ((2.0 * held - square) * valid(i, s)).astype(BF16)
        down.wait()
        here = slice(n * BS, (n + 1) * BS)
        for j in range(n + 1, ROWS):
            there = slice(j * BS, (j + 1) * BS)
            s = j - n - 1
            held = left[here, there].astype(F32)
            square = outer[here, there] + pd_in[here, there].astype(F32)
            dens[n, s] = ((2.0 * held - square) * valid(n, s)).astype(BF16)

    others = e_out.at[pl.ds(0, GROUP - 1)]
    pltpu.make_async_copy(others, others, en_send).wait()
    pltpu.make_async_copy(others, others, en_recv).wait()
    energies[...] = jnp.sum(e_in[...], axis=0) * DENSITY_SCALE * atoms[mine, pl.ds(12, 4), :]


def on_device(density, block_mask, orbital_cell, slab_of_device, positions, charges):
    dma = pltpu.SemaphoreType.DMA
    new_density, energies = pl.pallas_call(
        kernel,
        out_shape=(
            pltpu.VMEM((ROWS, SLOTS, BS, BS), BF16),
            pltpu.VMEM((4, BS), F32),
        ),
        in_specs=[
            pl.BlockSpec(memory_space=pl.ANY),
            pl.BlockSpec(memory_space=pltpu.SMEM),
            pl.BlockSpec(memory_space=pltpu.SMEM),
            pl.BlockSpec(memory_space=pltpu.VMEM),
            pl.BlockSpec(memory_space=pltpu.VMEM),
            pl.BlockSpec(memory_space=pltpu.VMEM),
        ],
        out_specs=(pl.BlockSpec(memory_space=pltpu.VMEM), pl.BlockSpec(memory_space=pltpu.VMEM)),
        scratch_shapes=[
            pltpu.VMEM((SPAN, 3 * SPAN), BF16),
            pltpu.VMEM((3 * SPAN, SPAN), BF16),
            pltpu.VMEM((SPAN, SPAN), F32),
            pltpu.VMEM((SPAN, SPAN), BF16),
            pltpu.VMEM((SPAN, SPAN), BF16),
            pltpu.VMEM((SPAN, SPAN), BF16),
            pltpu.VMEM((SPAN, SPAN), BF16),
            pltpu.VMEM((GROUP, 16, BS), F32),
            pltpu.VMEM((2 * GRID, ATOMS_HERE), BF16),
            pltpu.VMEM((GRID, ATOMS_HERE), F32),
            pltpu.VMEM((RING * GRID, ATOMS_DEV), BF16),
            pltpu.VMEM((RING * GRID, 2 * GRID), F32),
            pltpu.VMEM((RING, GRID, GRID), F32),
            pltpu.VMEM((RING, GRID, GRID), F32),
            pltpu.VMEM((RING, GRID, GRID), BF16),
            pltpu.VMEM((GROUP, 4, BS), F32),
            pltpu.VMEM((GROUP, 4, BS), F32),
            dma((ROWS,)),
            dma((2,)),
            dma((2, ROWS)),
            dma((2, ROWS)),
            dma((2, ROWS)),
            dma((2, ROWS)),
            dma((RING,)),
            dma((RING,)),
            dma((RING,)),
            dma((RING,)),
            dma,
            dma,
        ],
        compiler_params=pltpu.CompilerParams(
            collective_id=0, has_side_effects=True, vmem_limit_bytes=52 * 1024 * 1024
        ),
        cost_estimate=pl.CostEstimate(flops=10**10, bytes_accessed=10**7, transcendentals=4 * 10**6),
        name="purify",
    )(density, block_mask, slab_of_device, orbital_cell.reshape(ROWS, BS), positions, charges.reshape(4, BS))
    return new_density, energies.reshape(ATOMS_DEV)


def solution(mesh):
    in_specs = (
        P(("grp", "row", "col"), None, None, None),
        P(("grp", "row", "col"), None),
        P(("grp", "row", "col")),
        P(),
        P(None, ("grp", "row", "col")),
        P(("grp", "row", "col")),
    )
    out_specs = (P(("grp", "row", "col"), None, None, None), P(("grp", "row", "col")))
    return jax.shard_map(
        on_device, mesh=mesh, in_specs=in_specs, out_specs=out_specs, check_vma=False
    )
```

```python
import functools
import math

import jax
import jax.numpy as jnp
from jax import lax
from jax.experimental import pallas as pl
from jax.experimental.pallas import tpu as pltpu
from jax.sharding import PartitionSpec as P

BS = 128
BAND = 7
SLOTS = 15
ROWS = 8
NBLOCKS = 1024
DEVICES = 128
GRID = 128
SPAN = ROWS * BS
GROUP = 32
RING = 4
ATOMS_DEV = 512
ATOMS_HERE = GROUP * ATOMS_DEV

COUPLE = 0.5
DENSITY_SCALE = 0.05
ROOT = math.sqrt(math.log2(math.e) / 8.0)

MESH = pl.DeviceIdType.MESH
F32 = jnp.float32
BF16 = jnp.bfloat16


def dot(a, b):
    return jnp.dot(a, b, preferred_element_type=F32)


def dot_nt(a, b):
    return lax.dot_general(a, b, (((1,), (1,)), ((), ())), preferred_element_type=F32)


def bell(points, centre):
    offset = points - centre
    return jnp.exp2(-(offset * offset))


def kernel(
    density, mask, slabs, cells, positions, charges, dens, energies,
    left, right, outer, pu_out, pd_out, pu_in, pd_in,
    atoms, tab_y, tab_z, lhs, pot_acc, pot_out, pot_in, rho, e_out, e_in,
    dens_sem, gather_sem, halo_send, halo_recv, part_send, part_recv,
    pot_send, pot_recv, rho_send, rho_recv, en_send, en_recv,
):
    g, r, c = lax.axis_index("grp"), lax.axis_index("row"), lax.axis_index("col")
    me = (g * 8 + r) * 4 + c
    half, z = r // 4, r % 4
    mine = (g * 2 + half) * 4 + c

    def coords(index):
        return (index // 32, (index // 4) % 8, index % 4)

    after = coords((me + 1) % DEVICES)
    before = coords((me + DEVICES - 1) % DEVICES)

    def place(slot):
        return (slot // 8, ((slot // 4) % 2) * 4 + z, slot % 4)

    def peer(k):
        slot = (mine + k) % GROUP
        return slot, place(slot)

    def ring(k):
        return (g, half * 4 + (z + k) % RING, c)

    loads = [
        pltpu.make_async_copy(density.at[i], dens.at[i], dens_sem.at[i]) for i in range(ROWS)
    ]
    outside_in = (7, 0, 6, 1, 5, 2, 4, 3)
    for i in outside_in:
        loads[i].start()
    for j in range(4):
        for d in range(3):
            atoms[mine, pl.ds(4 * d + j, 1), :] = positions[d:d + 1, j * BS:(j + 1) * BS]
        atoms[mine, pl.ds(12 + j, 1), :] = charges[j:j + 1, :]

    barrier = pltpu.get_barrier_semaphore()

    @pl.loop(1, GROUP)
    def _(k):
        pl.semaphore_signal(barrier, inc=1, device_id=peer(k)[1], device_id_type=MESH)

    for k in range(1, RING):
        pl.semaphore_signal(barrier, inc=1, device_id=ring(k), device_id_type=MESH)
    pl.semaphore_signal(barrier, inc=1, device_id=after, device_id_type=MESH)
    pl.semaphore_signal(barrier, inc=1, device_id=before, device_id_type=MESH)
    pl.semaphore_wait(barrier, GROUP - 1 + RING - 1 + 2)

    @pl.loop(1, GROUP)
    def _(k):
        pltpu.make_async_remote_copy(
            atoms.at[mine], atoms.at[mine], gather_sem.at[0], gather_sem.at[1],
            device_id=peer(k)[1], device_id_type=MESH,
        ).start()

    zero = jnp.zeros((BS, BS), BF16)
    for a in range(0, ROWS, 2):
        for i, j in ((a, a), (a, a + 1), (a + 1, a), (a + 1, a + 1)):
            if j >= i:
                left[i * BS:(i + 1) * BS, 2 * SPAN + j * BS:2 * SPAN + (j + 1) * BS] = zero
                right[i * BS:(i + 1) * BS, j * BS:(j + 1) * BS] = zero
            if j <= i:
                left[i * BS:(i + 1) * BS, j * BS:(j + 1) * BS] = zero
                right[2 * SPAN + i * BS:2 * SPAN + (i + 1) * BS, j * BS:(j + 1) * BS] = zero

    def valid(i, s):
        column = me * ROWS + (i + s - BAND)
        inside = jnp.logical_and(column >= 0, column < NBLOCKS)
        return (mask[i, s] * inside.astype(jnp.int32)).astype(F32)

    to_next, to_prev = {}, {}
    for i in outside_in:
        loads[i].wait()
        for s in range(SLOTS):
            k = i + s + 1
            block = (dens[i, s].astype(F32) * valid(i, s)).astype(BF16)
            left[i * BS:(i + 1) * BS, k * BS:(k + 1) * BS] = block
            if ROWS <= k < 2 * ROWS:
                right[SPAN + i * BS:SPAN + (i + 1) * BS, (k - ROWS) * BS:(k - ROWS + 1) * BS] = block
        here = pl.ds(i * BS, BS)
        if i > 0:
            copy = pltpu.make_async_remote_copy(
                left.at[here, pl.ds(2 * SPAN, i * BS)], right.at[here, pl.ds(0, i * BS)],
                halo_send.at[0, i], halo_recv.at[0, i], device_id=after, device_id_type=MESH,
            )
            copy.start()
            to_next[i] = copy
        if i < ROWS - 1:
            there = pl.ds((i + 1) * BS, (ROWS - 1 - i) * BS)
            copy = pltpu.make_async_remote_copy(
                left.at[here, there], right.at[pl.ds(2 * SPAN + i * BS, BS), there],
                halo_send.at[1, i], halo_recv.at[1, i], device_id=before, device_id_type=MESH,
            )
            copy.start()
            to_prev[i] = copy

    others = atoms.at[pl.ds(0, GROUP - 1)]
    pltpu.make_async_copy(others, others, gather_sem.at[0]).wait()
    pltpu.make_async_copy(others, others, gather_sem.at[1]).wait()

    points = lax.broadcasted_iota(jnp.int32, (GRID, BS), 0).astype(F32) * ROOT
    first = me - 4 * z
    planes = [slabs[first + 4 * p].astype(F32) * ROOT for p in range(RING)]
    pot_acc[...] = jnp.zeros_like(pot_acc)

    def tables(slot):
        ys, ws = [], []
        for j in range(4):
            at = pl.ds(pl.multiple_of(slot * ATOMS_DEV + j * BS, BS), BS)
            centre = [atoms[slot, pl.ds(4 * d + j, 1), :] * (GRID * ROOT) for d in range(3)]
            charge = atoms[slot, pl.ds(12 + j, 1), :]
            along_y = bell(points, centre[1])
            high = along_y.astype(BF16)
            low = (along_y - high.astype(F32)).astype(BF16)
            tab_y[0:GRID, at] = high
            tab_y[GRID:2 * GRID, at] = low
            ys.append(jnp.concatenate([high, low], axis=0))
            along_z = bell(points, centre[2])
            tab_z[:, at] = along_z
            ws.append(jnp.concatenate([
                (along_z * (bell(planes[p], centre[0]) * charge)).astype(BF16) for p in range(RING)
            ], axis=0))
        return jnp.concatenate(ws, axis=1), jnp.concatenate(ys, axis=1)

    def partial_potential(start, stop):
        @pl.loop(start, stop)
        def _(t):
            ones = tables(2 * t)
            twos = tables(2 * t + 1)
            pot_acc[...] += dot_nt(*ones) + dot_nt(*twos)

    pairs = []

    def corners(n):
        i = BAND - n
        here, there = pl.ds(i * BS, BS), pl.ds(0, i * BS)
        pu_out[here, there] = dot(
            right[i * BS:(i + 1) * BS, 0:i * BS], right[SPAN:SPAN + i * BS, 0:i * BS]
        ).astype(BF16)
        up = pltpu.make_async_remote_copy(
            pu_out.at[here, there], pu_in.at[here, there],
            part_send.at[0, i], part_recv.at[0, i], device_id=before, device_id_type=MESH,
        )
        start = (n + 1) * BS
        here, there = pl.ds(n * BS, BS), pl.ds(start, SPAN - start)
        pd_out[here, there] = dot(
            right[2 * SPAN + n * BS:2 * SPAN + (n + 1) * BS, start:SPAN],
            right[SPAN + start:2 * SPAN, start:SPAN],
        ).astype(BF16)
        down = pltpu.make_async_remote_copy(
            pd_out.at[here, there], pd_in.at[here, there],
            part_send.at[1, n], part_recv.at[1, n], device_id=after, device_id_type=MESH,
        )
        pairs.append((up, down))

    def start_pair(n):
        for copy in pairs[n]:
            copy.start()

    def halo_pair(n):
        to_next[BAND - n].wait()
        to_prev[n].wait()

    partial_potential(0, GROUP // 2)

    for p in range(RING):
        part = pot_acc[p * GRID:(p + 1) * GRID, 0:GRID] + pot_acc[p * GRID:(p + 1) * GRID, GRID:2 * GRID]
        pot_out[p] = part
    pot_copies = []
    for k in range(1, RING):
        target = (z + k) % RING
        copy = pltpu.make_async_remote_copy(
            pot_out.at[target], pot_in.at[k], pot_send.at[k], pot_recv.at[k],
            device_id=ring(k), device_id_type=MESH,
        )
        copy.start()
        pot_copies.append(copy)
    potential = pot_out[z]
    for k, copy in zip(range(1, RING), pot_copies):
        copy.wait()
        potential = potential + pot_in[k]

    high = potential.astype(BF16)
    both = jnp.concatenate([high, (potential - high.astype(F32)).astype(BF16)], axis=1)
    cell_y = lax.shift_right_logical(cells[...], 7)
    cell_z = jnp.bitwise_and(cells[...], GRID - 1)
    height = lax.broadcasted_iota(jnp.int32, (GRID, BS), 0)
    eye = (height == lax.broadcasted_iota(jnp.int32, (GRID, BS), 1)).astype(F32)

    def hot(cell, i):
        return (height == cell[i:i + 1, :]).astype(F32)

    for i in range(ROWS):
        hot_y = hot(cell_y, i).astype(BF16)
        rows = dot(both, jnp.concatenate([hot_y, hot_y], axis=0))
        shift = COUPLE * jnp.sum(rows * hot(cell_z, i), axis=0, keepdims=True)
        block = ((dens[i, BAND].astype(F32) - shift * eye) * valid(i, BAND)).astype(BF16)
        left[i * BS:(i + 1) * BS, SPAN + i * BS:SPAN + (i + 1) * BS] = block
        right[SPAN + i * BS:SPAN + (i + 1) * BS, i * BS:(i + 1) * BS] = block

    halo_pair(0)
    corners(0)
    for n in range(1, BAND):
        halo_pair(n)
    start_pair(0)

    def middle(a, b):
        first, last = max(a, b) + 1, min(a, b) + 16
        window = slice(first * BS, (last + 1) * BS)
        total = dot(left[a * BS:(a + 2) * BS, window], right[window, b * BS:(b + 2) * BS])
        for i in (a, a + 1):
            for j in (b, b + 1):
                s = j - i + BAND
                held = left[i * BS:(i + 1) * BS, SPAN + j * BS:SPAN + (j + 1) * BS].astype(F32)
                square = total[(i - a) * BS:(i - a + 1) * BS, (j - b) * BS:(j - b + 1) * BS]
                dens[i, s] = ((2.0 * held - square) * valid(i, s)).astype(BF16)

    for a in range(0, ROWS, 2):
        middle(a, a)

    grid_here = jnp.zeros((GRID, GRID), F32)
    for i in range(ROWS):
        diagonal = jnp.sum(dens[i, BAND].astype(F32) * eye, axis=0, keepdims=True)
        spread = (hot(cell_z, i) * diagonal).astype(BF16)
        grid_here = grid_here + dot_nt(spread, hot(cell_y, i).astype(BF16))
    rho[0] = grid_here.astype(BF16)
    rho_copies = []
    for k in range(1, RING):
        copy = pltpu.make_async_remote_copy(
            rho.at[0], rho.at[k], rho_send.at[k], rho_recv.at[k],
            device_id=ring(k), device_id_type=MESH,
        )
        copy.start()
        rho_copies.append(copy)
    for n in range(1, BAND):
        corners(n)
    for copy in rho_copies:
        copy.wait()
    for n in range(1, BAND):
        start_pair(n)

    for a in range(0, ROWS, 2):
        for b in range(0, ROWS, 2):
            if a != b:
                middle(a, b)
    for b in range(0, ROWS, 2):
        columns = slice(b * BS, (b + 2) * BS)
        rows = slice((b + 1) * BS, SPAN)
        outer[rows, columns] = dot(
            left[rows, SPAN + b * BS:2 * SPAN],
            left[b * BS:SPAN, 2 * SPAN + b * BS:2 * SPAN + (b + 2) * BS],
        )
        rows = slice(0, (b + 1) * BS)
        outer[rows, columns] = dot(
            left[rows, SPAN:SPAN + (b + 2) * BS], left[0:(b + 2) * BS, b * BS:(b + 2) * BS]
        )


    order = [(z - k + RING) % RING for k in range(RING)]
    mine_planes = [slabs[first + 4 * order[k]].astype(F32) * ROOT for k in range(RING)]
    weights = jnp.concatenate([rho[k] for k in range(RING)], axis=0)
    lhs[:, 0:GRID] = weights
    lhs[:, GRID:2 * GRID] = weights

    @pl.loop(0, GROUP)
    def _(k):
        slot = (mine + 1 + k) % GROUP
        base = pl.multiple_of(slot * ATOMS_DEV, ATOMS_DEV)
        inner = dot(lhs[:, 0:2 * GRID], tab_y[:, pl.ds(base, ATOMS_DEV)])
        for j in range(4):
            at = pl.ds(base + j * BS, BS)
            centre = atoms[slot, pl.ds(j, 1), :] * (GRID * ROOT)
            along_z = tab_z[:, at]
            total = jnp.zeros((1, BS), F32)
            for p in range(RING):
                piece = inner[p * GRID:(p + 1) * GRID, j * BS:(j + 1) * BS]
                total += bell(mine_planes[p], centre) * jnp.sum(piece * along_z, axis=0, keepdims=True)
            e_out[slot, pl.ds(j, 1), :] = total

        @pl.when(k < GROUP - 1)
        def _():
            pltpu.make_async_remote_copy(
                e_out.at[slot], e_in.at[mine], en_send, en_recv,
                device_id=place(slot), device_id_type=MESH,
            ).start()

    e_in[mine] = e_out[mine]

    for n in range(BAND):
        up, down = pairs[n]
        up.wait()
        i = BAND - n
        here = slice(i * BS, (i + 1) * BS)
        for j in range(i):
            there = slice(j * BS, (j + 1) * BS)
            s = j - i + SLOTS
            held = left[here, 2 * SPAN + j * BS:2 * SPAN + (j + 1) * BS].astype(F32)
            square = outer[here, there] + pu_in[here, there].astype(F32)
            dens[i, s] = ((2.0 * held - square) * valid(i, s)).astype(BF16)
        down.wait()
        here = slice(n * BS, (n + 1) * BS)
        for j in range(n + 1, ROWS):
            there = slice(j * BS, (j + 1) * BS)
            s = j - n - 1
            held = left[here, there].astype(F32)
            square = outer[here, there] + pd_in[here, there].astype(F32)
            dens[n, s] = ((2.0 * held - square) * valid(n, s)).astype(BF16)

    others = e_out.at[pl.ds(0, GROUP - 1)]
    pltpu.make_async_copy(others, others, en_send).wait()
    pltpu.make_async_copy(others, others, en_recv).wait()
    energies[...] = jnp.sum(e_in[...], axis=0) * DENSITY_SCALE * atoms[mine, pl.ds(12, 4), :]


def on_device(density, block_mask, orbital_cell, slab_of_device, positions, charges):
    dma = pltpu.SemaphoreType.DMA
    new_density, energies = pl.pallas_call(
        kernel,
        out_shape=(
            pltpu.VMEM((ROWS, SLOTS, BS, BS), BF16),
            pltpu.VMEM((4, BS), F32),
        ),
        in_specs=[
            pl.BlockSpec(memory_space=pl.ANY),
            pl.BlockSpec(memory_space=pltpu.SMEM),
            pl.BlockSpec(memory_space=pltpu.SMEM),
            pl.BlockSpec(memory_space=pltpu.VMEM),
            pl.BlockSpec(memory_space=pltpu.VMEM),
            pl.BlockSpec(memory_space=pltpu.VMEM),
        ],
        out_specs=(pl.BlockSpec(memory_space=pltpu.VMEM), pl.BlockSpec(memory_space=pltpu.VMEM)),
        scratch_shapes=[
            pltpu.VMEM((SPAN, 3 * SPAN), BF16),
            pltpu.VMEM((3 * SPAN, SPAN), BF16),
            pltpu.VMEM((SPAN, SPAN), F32),
            pltpu.VMEM((SPAN, SPAN), BF16),
            pltpu.VMEM((SPAN, SPAN), BF16),
            pltpu.VMEM((SPAN, SPAN), BF16),
            pltpu.VMEM((SPAN, SPAN), BF16),
            pltpu.VMEM((GROUP, 16, BS), F32),
            pltpu.VMEM((2 * GRID, ATOMS_HERE), BF16),
            pltpu.VMEM((GRID, ATOMS_HERE), F32),
            pltpu.VMEM((RING * GRID, ATOMS_DEV), BF16),
            pltpu.VMEM((RING * GRID, 2 * GRID), F32),
            pltpu.VMEM((RING, GRID, GRID), F32),
            pltpu.VMEM((RING, GRID, GRID), F32),
            pltpu.VMEM((RING, GRID, GRID), BF16),
            pltpu.VMEM((GROUP, 4, BS), F32),
            pltpu.VMEM((GROUP, 4, BS), F32),
            dma((ROWS,)),
            dma((2,)),
            dma((2, ROWS)),
            dma((2, ROWS)),
            dma((2, ROWS)),
            dma((2, ROWS)),
            dma((RING,)),
            dma((RING,)),
            dma((RING,)),
            dma((RING,)),
            dma,
            dma,
        ],
        compiler_params=pltpu.CompilerParams(
            collective_id=0, has_side_effects=True, vmem_limit_bytes=52 * 1024 * 1024
        ),
        cost_estimate=pl.CostEstimate(flops=10**10, bytes_accessed=10**7, transcendentals=4 * 10**6),
        name="purify",
    )(density, block_mask, slab_of_device, orbital_cell.reshape(ROWS, BS), positions, charges.reshape(4, BS))
    return new_density, energies.reshape(ATOMS_DEV)


def solution(mesh):
    in_specs = (
        P(("grp", "row", "col"), None, None, None),
        P(("grp", "row", "col"), None),
        P(("grp", "row", "col")),
        P(),
        P(None, ("grp", "row", "col")),
        P(("grp", "row", "col")),
    )
    out_specs = (P(("grp", "row", "col"), None, None, None), P(("grp", "row", "col")))
    return jax.shard_map(
        on_device, mesh=mesh, in_specs=in_specs, out_specs=out_specs, check_vma=False
    )
```

```python
import functools
import math

import jax
import jax.numpy as jnp
from jax import lax
from jax.experimental import pallas as pl
from jax.experimental.pallas import tpu as pltpu
from jax.sharding import PartitionSpec as P

BS = 128
BAND = 7
SLOTS = 15
ROWS = 8
NBLOCKS = 1024
DEVICES = 128
GRID = 128
SPAN = ROWS * BS
GROUP = 32
RING = 4
ATOMS_DEV = 512
ATOMS_HERE = GROUP * ATOMS_DEV

COUPLE = 0.5
DENSITY_SCALE = 0.05
ROOT = math.sqrt(math.log2(math.e) / 8.0)

MESH = pl.DeviceIdType.MESH
F32 = jnp.float32
BF16 = jnp.bfloat16


def dot(a, b):
    return jnp.dot(a, b, preferred_element_type=F32)


def dot_nt(a, b):
    return lax.dot_general(a, b, (((1,), (1,)), ((), ())), preferred_element_type=F32)


def bell(points, centre):
    offset = points - centre
    return jnp.exp2(-(offset * offset))


def kernel(
    density, mask, slabs, cells, positions, charges, dens, energies,
    left, right, outer, pu_out, pd_out, pu_in, pd_in,
    atoms, tab_y, tab_z, lhs, pot_acc, pot_out, pot_in, rho, e_out, e_in,
    dens_sem, gather_sem, halo_send, halo_recv, part_send, part_recv,
    pot_send, pot_recv, rho_send, rho_recv, en_send, en_recv,
):
    g, r, c = lax.axis_index("grp"), lax.axis_index("row"), lax.axis_index("col")
    me = (g * 8 + r) * 4 + c
    half, z = r // 4, r % 4
    mine = (g * 2 + half) * 4 + c

    def coords(index):
        return (index // 32, (index // 4) % 8, index % 4)

    after = coords((me + 1) % DEVICES)
    before = coords((me + DEVICES - 1) % DEVICES)

    def place(slot):
        return (slot // 8, ((slot // 4) % 2) * 4 + z, slot % 4)

    def peer(k):
        slot = (mine + k) % GROUP
        return slot, place(slot)

    def ring(k):
        return (g, half * 4 + (z + k) % RING, c)

    loads = [
        pltpu.make_async_copy(density.at[i], dens.at[i], dens_sem.at[i]) for i in range(ROWS)
    ]
    outside_in = (7, 0, 6, 1, 5, 2, 4, 3)
    for i in outside_in:
        loads[i].start()
    for j in range(4):
        for d in range(3):
            atoms[mine, pl.ds(4 * d + j, 1), :] = positions[d:d + 1, j * BS:(j + 1) * BS]
        atoms[mine, pl.ds(12 + j, 1), :] = charges[j:j + 1, :]

    barrier = pltpu.get_barrier_semaphore()

    @pl.loop(1, GROUP)
    def _(k):
        pl.semaphore_signal(barrier, inc=1, device_id=peer(k)[1], device_id_type=MESH)

    for k in range(1, RING):
        pl.semaphore_signal(barrier, inc=1, device_id=ring(k), device_id_type=MESH)
    pl.semaphore_signal(barrier, inc=1, device_id=after, device_id_type=MESH)
    pl.semaphore_signal(barrier, inc=1, device_id=before, device_id_type=MESH)
    pl.semaphore_wait(barrier, GROUP - 1 + RING - 1 + 2)

    @pl.loop(1, GROUP)
    def _(k):
        pltpu.make_async_remote_copy(
            atoms.at[mine], atoms.at[mine], gather_sem.at[0], gather_sem.at[1],
            device_id=peer(k)[1], device_id_type=MESH,
        ).start()

    zero = jnp.zeros((BS, BS), BF16)
    for a in range(0, ROWS, 2):
        for i, j in ((a, a), (a, a + 1), (a + 1, a), (a + 1, a + 1)):
            if j >= i:
                left[i * BS:(i + 1) * BS, 2 * SPAN + j * BS:2 * SPAN + (j + 1) * BS] = zero
                right[i * BS:(i + 1) * BS, j * BS:(j + 1) * BS] = zero
            if j <= i:
                left[i * BS:(i + 1) * BS, j * BS:(j + 1) * BS] = zero
                right[2 * SPAN + i * BS:2 * SPAN + (i + 1) * BS, j * BS:(j + 1) * BS] = zero

    def valid(i, s):
        column = me * ROWS + (i + s - BAND)
        inside = jnp.logical_and(column >= 0, column < NBLOCKS)
        return (mask[i, s] * inside.astype(jnp.int32)).astype(F32)

    to_next, to_prev = {}, {}
    for i in outside_in:
        loads[i].wait()
        for s in range(SLOTS):
            k = i + s + 1
            block = (dens[i, s].astype(F32) * valid(i, s)).astype(BF16)
            left[i * BS:(i + 1) * BS, k * BS:(k + 1) * BS] = block
            if ROWS <= k < 2 * ROWS:
                right[SPAN + i * BS:SPAN + (i + 1) * BS, (k - ROWS) * BS:(k - ROWS + 1) * BS] = block
        here = pl.ds(i * BS, BS)
        if i > 0:
            copy = pltpu.make_async_remote_copy(
                left.at[here, pl.ds(2 * SPAN, i * BS)], right.at[here, pl.ds(0, i * BS)],
                halo_send.at[0, i], halo_recv.at[0, i], device_id=after, device_id_type=MESH,
            )
            copy.start()
            to_next[i] = copy
        if i < ROWS - 1:
            there = pl.ds((i + 1) * BS, (ROWS - 1 - i) * BS)
            copy = pltpu.make_async_remote_copy(
                left.at[here, there], right.at[pl.ds(2 * SPAN + i * BS, BS), there],
                halo_send.at[1, i], halo_recv.at[1, i], device_id=before, device_id_type=MESH,
            )
            copy.start()
            to_prev[i] = copy

    others = atoms.at[pl.ds(0, GROUP - 1)]
    pltpu.make_async_copy(others, others, gather_sem.at[0]).wait()
    pltpu.make_async_copy(others, others, gather_sem.at[1]).wait()

    points = lax.broadcasted_iota(jnp.int32, (GRID, BS), 0).astype(F32) * ROOT
    first = me - 4 * z
    planes = [slabs[first + 4 * p].astype(F32) * ROOT for p in range(RING)]
    pot_acc[...] = jnp.zeros_like(pot_acc)

    def tables(slot):
        ys, ws = [], []
        for j in range(4):
            at = pl.ds(pl.multiple_of(slot * ATOMS_DEV + j * BS, BS), BS)
            centre = [atoms[slot, pl.ds(4 * d + j, 1), :] * (GRID * ROOT) for d in range(3)]
            charge = atoms[slot, pl.ds(12 + j, 1), :]
            along_y = bell(points, centre[1])
            high = along_y.astype(BF16)
            low = (along_y - high.astype(F32)).astype(BF16)
            tab_y[0:GRID, at] = high
            tab_y[GRID:2 * GRID, at] = low
            ys.append(jnp.concatenate([high, low], axis=0))
            along_z = bell(points, centre[2])
            tab_z[:, at] = along_z
            ws.append(jnp.concatenate([
                (along_z * (bell(planes[p], centre[0]) * charge)).astype(BF16) for p in range(RING)
            ], axis=0))
        return jnp.concatenate(ws, axis=1), jnp.concatenate(ys, axis=1)

    def partial_potential(start, stop):
        @pl.loop(start, stop)
        def _(t):
            ones = tables(2 * t)
            twos = tables(2 * t + 1)
            pot_acc[...] += dot_nt(*ones) + dot_nt(*twos)

    pairs = []

    def corners(n):
        i = BAND - n
        here, there = pl.ds(i * BS, BS), pl.ds(0, i * BS)
        pu_out[here, there] = dot(
            right[i * BS:(i + 1) * BS, 0:i * BS], right[SPAN:SPAN + i * BS, 0:i * BS]
        ).astype(BF16)
        up = pltpu.make_async_remote_copy(
            pu_out.at[here, there], pu_in.at[here, there],
            part_send.at[0, i], part_recv.at[0, i], device_id=before, device_id_type=MESH,
        )
        start = (n + 1) * BS
        here, there = pl.ds(n * BS, BS), pl.ds(start, SPAN - start)
        pd_out[here, there] = dot(
            right[2 * SPAN + n * BS:2 * SPAN + (n + 1) * BS, start:SPAN],
            right[SPAN + start:2 * SPAN, start:SPAN],
        ).astype(BF16)
        down = pltpu.make_async_remote_copy(
            pd_out.at[here, there], pd_in.at[here, there],
            part_send.at[1, n], part_recv.at[1, n], device_id=after, device_id_type=MESH,
        )
        pairs.append((up, down))

    def start_pair(n):
        for copy in pairs[n]:
            copy.start()

    def halo_pair(n):
        to_next[BAND - n].wait()
        to_prev[n].wait()

    partial_potential(0, GROUP // 2)

    for p in range(RING):
        part = pot_acc[p * GRID:(p + 1) * GRID, 0:GRID] + pot_acc[p * GRID:(p + 1) * GRID, GRID:2 * GRID]
        pot_out[p] = part
    pot_copies = []
    for k in range(1, RING):
        target = (z + k) % RING
        copy = pltpu.make_async_remote_copy(
            pot_out.at[target], pot_in.at[k], pot_send.at[k], pot_recv.at[k],
            device_id=ring(k), device_id_type=MESH,
        )
        copy.start()
        pot_copies.append(copy)
    potential = pot_out[z]
    for k, copy in zip(range(1, RING), pot_copies):
        copy.wait()
        potential = potential + pot_in[k]

    high = potential.astype(BF16)
    both = jnp.concatenate([high, (potential - high.astype(F32)).astype(BF16)], axis=1)
    cell_y = lax.shift_right_logical(cells[...], 7)
    cell_z = jnp.bitwise_and(cells[...], GRID - 1)
    height = lax.broadcasted_iota(jnp.int32, (GRID, BS), 0)
    eye = (height == lax.broadcasted_iota(jnp.int32, (GRID, BS), 1)).astype(F32)

    def hot(cell, i):
        return (height == cell[i:i + 1, :]).astype(F32)

    for i in range(ROWS):
        hot_y = hot(cell_y, i).astype(BF16)
        rows = dot(both, jnp.concatenate([hot_y, hot_y], axis=0))
        shift = COUPLE * jnp.sum(rows * hot(cell_z, i), axis=0, keepdims=True)
        block = ((dens[i, BAND].astype(F32) - shift * eye) * valid(i, BAND)).astype(BF16)
        left[i * BS:(i + 1) * BS, SPAN + i * BS:SPAN + (i + 1) * BS] = block
        right[SPAN + i * BS:SPAN + (i + 1) * BS, i * BS:(i + 1) * BS] = block

    for a in range(0, ROWS, 2):
        own = slice(a * BS, (a + 2) * BS)
        outer[own, own] = dot(left[own, SPAN:2 * SPAN], right[SPAN:2 * SPAN, own])
    for n in range(BAND):
        halo_pair(n)
        corners(n)
    start_pair(0)

    def middle(a, b):
        first, last = max(a, b) + 1, min(a, b) + 16
        window = slice(first * BS, (last + 1) * BS)
        rows, columns = slice(a * BS, (a + 2) * BS), slice(b * BS, (b + 2) * BS)
        if a == b:
            total = outer[rows, columns]
            for window in (slice(first * BS, SPAN), slice(2 * SPAN, (last + 1) * BS)):
                total = total + dot(left[rows, window], right[window, columns])
        else:
            total = dot(left[rows, window], right[window, columns])
        for i in (a, a + 1):
            for j in (b, b + 1):
                s = j - i + BAND
                held = left[i * BS:(i + 1) * BS, SPAN + j * BS:SPAN + (j + 1) * BS].astype(F32)
                square = total[(i - a) * BS:(i - a + 1) * BS, (j - b) * BS:(j - b + 1) * BS]
                dens[i, s] = ((2.0 * held - square) * valid(i, s)).astype(BF16)

    for a in range(0, ROWS, 2):
        middle(a, a)

    grid_here = jnp.zeros((GRID, GRID), F32)
    for i in range(ROWS):
        diagonal = jnp.sum(dens[i, BAND].astype(F32) * eye, axis=0, keepdims=True)
        spread = (hot(cell_z, i) * diagonal).astype(BF16)
        grid_here = grid_here + dot_nt(spread, hot(cell_y, i).astype(BF16))
    rho[0] = grid_here.astype(BF16)
    rho_copies = []
    for k in range(1, RING):
        copy = pltpu.make_async_remote_copy(
            rho.at[0], rho.at[k], rho_send.at[k], rho_recv.at[k],
            device_id=ring(k), device_id_type=MESH,
        )
        copy.start()
        rho_copies.append(copy)
    for copy in rho_copies:
        copy.wait()
    for n in range(1, BAND):
        start_pair(n)

    for a in range(0, ROWS, 2):
        for b in range(0, ROWS, 2):
            if a != b:
                middle(a, b)
    for b in range(0, ROWS, 2):
        columns = slice(b * BS, (b + 2) * BS)
        rows = slice((b + 1) * BS, SPAN)
        outer[rows, columns] = dot(
            left[rows, SPAN + b * BS:2 * SPAN],
            left[b * BS:SPAN, 2 * SPAN + b * BS:2 * SPAN + (b + 2) * BS],
        )
        rows = slice(0, (b + 1) * BS)
        outer[rows, columns] = dot(
            left[rows, SPAN:SPAN + (b + 2) * BS], left[0:(b + 2) * BS, b * BS:(b + 2) * BS]
        )


    order = [(z - k + RING) % RING for k in range(RING)]
    mine_planes = [slabs[first + 4 * order[k]].astype(F32) * ROOT for k in range(RING)]
    weights = jnp.concatenate([rho[k] for k in range(RING)], axis=0)
    lhs[:, 0:GRID] = weights
    lhs[:, GRID:2 * GRID] = weights

    @pl.loop(0, GROUP)
    def _(k):
        slot = (mine + 1 + k) % GROUP
        base = pl.multiple_of(slot * ATOMS_DEV, ATOMS_DEV)
        inner = dot(lhs[:, 0:2 * GRID], tab_y[:, pl.ds(base, ATOMS_DEV)])
        for j in range(4):
            at = pl.ds(base + j * BS, BS)
            centre = atoms[slot, pl.ds(j, 1), :] * (GRID * ROOT)
            along_z = tab_z[:, at]
            total = jnp.zeros((1, BS), F32)
            for p in range(RING):
                piece = inner[p * GRID:(p + 1) * GRID, j * BS:(j + 1) * BS]
                total += bell(mine_planes[p], centre) * jnp.sum(piece * along_z, axis=0, keepdims=True)
            e_out[slot, pl.ds(j, 1), :] = total

        @pl.when(k < GROUP - 1)
        def _():
            pltpu.make_async_remote_copy(
                e_out.at[slot], e_in.at[mine], en_send, en_recv,
                device_id=place(slot), device_id_type=MESH,
            ).start()

    e_in[mine] = e_out[mine]

    for n in range(BAND):
        up, down = pairs[n]
        up.wait()
        i = BAND - n
        here = slice(i * BS, (i + 1) * BS)
        for j in range(i):
            there = slice(j * BS, (j + 1) * BS)
            s = j - i + SLOTS
            held = left[here, 2 * SPAN + j * BS:2 * SPAN + (j + 1) * BS].astype(F32)
            square = outer[here, there] + pu_in[here, there].astype(F32)
            dens[i, s] = ((2.0 * held - square) * valid(i, s)).astype(BF16)
        down.wait()
        here = slice(n * BS, (n + 1) * BS)
        for j in range(n + 1, ROWS):
            there = slice(j * BS, (j + 1) * BS)
            s = j - n - 1
            held = left[here, there].astype(F32)
            square = outer[here, there] + pd_in[here, there].astype(F32)
            dens[n, s] = ((2.0 * held - square) * valid(n, s)).astype(BF16)

    others = e_out.at[pl.ds(0, GROUP - 1)]
    pltpu.make_async_copy(others, others, en_send).wait()
    pltpu.make_async_copy(others, others, en_recv).wait()
    energies[...] = jnp.sum(e_in[...], axis=0) * DENSITY_SCALE * atoms[mine, pl.ds(12, 4), :]


def on_device(density, block_mask, orbital_cell, slab_of_device, positions, charges):
    dma = pltpu.SemaphoreType.DMA
    new_density, energies = pl.pallas_call(
        kernel,
        out_shape=(
            pltpu.VMEM((ROWS, SLOTS, BS, BS), BF16),
            pltpu.VMEM((4, BS), F32),
        ),
        in_specs=[
            pl.BlockSpec(memory_space=pl.ANY),
            pl.BlockSpec(memory_space=pltpu.SMEM),
            pl.BlockSpec(memory_space=pltpu.SMEM),
            pl.BlockSpec(memory_space=pltpu.VMEM),
            pl.BlockSpec(memory_space=pltpu.VMEM),
            pl.BlockSpec(memory_space=pltpu.VMEM),
        ],
        out_specs=(pl.BlockSpec(memory_space=pltpu.VMEM), pl.BlockSpec(memory_space=pltpu.VMEM)),
        scratch_shapes=[
            pltpu.VMEM((SPAN, 3 * SPAN), BF16),
            pltpu.VMEM((3 * SPAN, SPAN), BF16),
            pltpu.VMEM((SPAN, SPAN), F32),
            pltpu.VMEM((SPAN, SPAN), BF16),
            pltpu.VMEM((SPAN, SPAN), BF16),
            pltpu.VMEM((SPAN, SPAN), BF16),
            pltpu.VMEM((SPAN, SPAN), BF16),
            pltpu.VMEM((GROUP, 16, BS), F32),
            pltpu.VMEM((2 * GRID, ATOMS_HERE), BF16),
            pltpu.VMEM((GRID, ATOMS_HERE), F32),
            pltpu.VMEM((RING * GRID, ATOMS_DEV), BF16),
            pltpu.VMEM((RING * GRID, 2 * GRID), F32),
            pltpu.VMEM((RING, GRID, GRID), F32),
            pltpu.VMEM((RING, GRID, GRID), F32),
            pltpu.VMEM((RING, GRID, GRID), BF16),
            pltpu.VMEM((GROUP, 4, BS), F32),
            pltpu.VMEM((GROUP, 4, BS), F32),
            dma((ROWS,)),
            dma((2,)),
            dma((2, ROWS)),
            dma((2, ROWS)),
            dma((2, ROWS)),
            dma((2, ROWS)),
            dma((RING,)),
            dma((RING,)),
            dma((RING,)),
            dma((RING,)),
            dma,
            dma,
        ],
        compiler_params=pltpu.CompilerParams(
            collective_id=0, has_side_effects=True, vmem_limit_bytes=52 * 1024 * 1024
        ),
        cost_estimate=pl.CostEstimate(flops=10**10, bytes_accessed=10**7, transcendentals=4 * 10**6),
        name="purify",
    )(density, block_mask, slab_of_device, orbital_cell.reshape(ROWS, BS), positions, charges.reshape(4, BS))
    return new_density, energies.reshape(ATOMS_DEV)


def solution(mesh):
    in_specs = (
        P(("grp", "row", "col"), None, None, None),
        P(("grp", "row", "col"), None),
        P(("grp", "row", "col")),
        P(),
        P(None, ("grp", "row", "col")),
        P(("grp", "row", "col")),
    )
    out_specs = (P(("grp", "row", "col"), None, None, None), P(("grp", "row", "col")))
    return jax.shard_map(
        on_device, mesh=mesh, in_specs=in_specs, out_specs=out_specs, check_vma=False
    )
```
